32 devices in a mesh: dp: 4 (over x, core), tm: 4 (over z), space: 2 (over y).
Axes of the slice: x: 2, y: 2, z: 4, core: 2. Of those that a mesh axis runs over, the one named last changes fastest.
Arguments:
- feats: bfloat16 [4, 4, 16, 128, 256], P('dp', 'tm', 'space'), may hold values from -6 to 6
- w_spatial: bfloat16 [3, 3, 256, 256], replicated, may hold values from -0.125 to 0.125
- w_temporal: bfloat16 [768, 256], replicated, may hold values from -0.21875 to 0.21875
- teacher_mid: bfloat16 [4, 4, 16, 128, 256], P('dp', 'tm', 'space'), may hold values from -6 to 6
- w_down: bfloat16 [2, 2, 256, 512], replicated, may hold values from -0.1875 to 0.1875
- w_query: bfloat16 [512, 512], replicated, may hold values from -8 to 8
- w_key: bfloat16 [512, 512], replicated, may hold values from -1 to 1
- w_value: bfloat16 [512, 512], replicated, may hold values from -0.25 to 0.25
- w_out: bfloat16 [512, 512], replicated, may hold values from -0.25 to 0.25
- teacher_top: bfloat16 [4, 4, 8, 64, 512], P('dp', 'tm', 'space'), may hold values from -6 to 6
Outputs:
- student_top: bfloat16 [4, 4, 8, 64, 512], P('dp', 'tm', 'space')
- grad_temporal: float32 [768, 256], P(('tm', 'space'))
- grad_out: float32 [512, 512], P(('tm', 'space'))
The draws below stay inside these ranges and needn't reach their ends.
All inputs are finite; a program needn't handle non-finite values.
Results may differ from the reference program's by a relative error of at most 0.0075.
Values may be sent and summed in bfloat16 or wider, within the bound.
A program may use at most 64 MiB of HBM per device.

```python
import math
import jax
import jax.numpy as jnp
from jax import lax

C1 = 256
C2 = 512
KT = 3
W = 128
CLIPS = 4
FRAMES = 4
ROWS = 16


def paired_projections(key):
    base = jax.random.fold_in(key, 7)
    key_raw = jnp.clip(jax.random.normal(jax.random.fold_in(base, 1), (C2, C2), jnp.float32), -4.0, 4.0)
    query_raw = jnp.clip(jax.random.normal(jax.random.fold_in(base, 2), (C2, C2), jnp.float32), -4.0, 4.0)
    key_mat = key_raw / math.sqrt(C2)
    query_mat = query_raw / math.sqrt(C2)
    return (query_mat, key_mat)


def draw_w_query(key, part):
    return paired_projections(key)[0].astype(jnp.bfloat16)


def draw_w_key(key, part):
    return paired_projections(key)[1].astype(jnp.bfloat16)


def level_of(key, dims, pieces, smallest, high):
    def one(position, blocks):
        draws = jax.random.uniform(jax.random.fold_in(jax.random.fold_in(key, 6), position), (blocks,), jnp.float32, smallest / len(pieces), high / len(pieces))
        return jnp.repeat(jnp.exp(draws), dims[position] // blocks).reshape((-1,) + (1,) * (len(dims) - position - 1))

    level = one(*pieces[0])
    for cut in pieces[1:]:
        level = level * one(*cut)
    return level


def centred(stream_key, shape, deviation, limit, split=(), held_as=jnp.bfloat16):
    loudness = level_of(stream_key, shape, split, -0.22, 0.18) if split else 1.0
    drawn = jax.random.normal(stream_key, shape, jnp.float32) * deviation * loudness
    return jnp.minimum(jnp.maximum(drawn, -limit), limit).astype(held_as)


def setup_inputs(seed: int = 0) -> dict:
    seeds = jax.random.split(jax.random.key(seed), 11)
    feats = centred(seeds[0], (CLIPS, FRAMES, ROWS, W, C1), 1.0, 6.0, ((0, 4), (1, 4), (2, 2)))
    w_spatial = centred(seeds[1], (3, 3, C1, C1), (9 * C1) ** -0.5, 0.125)
    w_temporal = centred(seeds[2], (KT * C1, C1), (KT * C1) ** -0.5, 0.21875)
    teacher_mid = centred(seeds[3], (CLIPS, FRAMES, ROWS, W, C1), 1.0, 6.0, ((0, 4), (1, 4), (2, 2)))
    w_down = centred(seeds[4], (2, 2, C1, C2), (4 * C1) ** -0.5, 0.1875)
    w_query = draw_w_query(jax.random.fold_in(seeds[10], 71), 0)
    w_key = draw_w_key(jax.random.fold_in(seeds[10], 71), 0)
    w_value = centred(seeds[7], (C2, C2), C2 ** -0.5, 0.25)
    w_out = centred(seeds[8], (C2, C2), C2 ** -0.5, 0.25)
    teacher_top = centred(seeds[9], (CLIPS, FRAMES, ROWS // 2, W // 2, C2), 1.0, 6.0, ((0, 4), (1, 4), (2, 2)))
    return dict(feats=feats, w_spatial=w_spatial, w_temporal=w_temporal, teacher_mid=teacher_mid, w_down=w_down, w_query=w_query, w_key=w_key, w_value=w_value, w_out=w_out, teacher_top=teacher_top)


def reference(feats, w_spatial, w_temporal, teacher_mid, w_down, w_query, w_key, w_value, w_out, teacher_top):
    clips, frames, rows, cols, chan = feats.shape
    numbers = ('NHWC', 'HWIO', 'NHWC')
    flat = feats.reshape(clips * frames, rows, cols, chan)
    conv = lax.conv_general_dilated(flat, w_spatial, (1, 1), ((1, 1), (1, 1)), dimension_numbers=numbers, preferred_element_type=jnp.float32)
    spatial = jax.nn.silu(conv).astype(jnp.bfloat16).reshape(clips, frames, rows, cols, chan)
    zero = jnp.zeros_like(spatial[:, :1])
    back_one = jnp.concatenate([zero, spatial[:, :-1]], 1)[:, :frames]
    back_two = jnp.concatenate([zero, zero, spatial[:, :-2]], 1)[:, :frames]
    stacked = jnp.concatenate([back_two, back_one, spatial], -1).reshape(-1, 3 * chan)
    temporal = jnp.dot(stacked, w_temporal, preferred_element_type=jnp.float32)
    mid = (feats.reshape(-1, chan).astype(jnp.float32) + temporal).astype(jnp.bfloat16)
    diff_mid = (mid.astype(jnp.float32) - teacher_mid.reshape(-1, chan).astype(jnp.float32)).astype(jnp.bfloat16)
    scale_mid = 1.0 / math.sqrt(stacked.shape[0])
    grad_temporal = jnp.dot(stacked.T, diff_mid, preferred_element_type=jnp.float32) * scale_mid
    coarse = lax.conv_general_dilated(mid.reshape(clips * frames, rows, cols, chan), w_down, (2, 2), 'VALID', dimension_numbers=numbers, preferred_element_type=jnp.float32).astype(jnp.bfloat16)
    width = coarse.shape[-1]
    coarse = coarse.reshape(-1, width)
    query = jnp.dot(coarse, w_query, preferred_element_type=jnp.float32).astype(jnp.bfloat16)
    key = jnp.dot(coarse, w_key, preferred_element_type=jnp.float32).astype(jnp.bfloat16)
    value = jnp.dot(coarse, w_value, preferred_element_type=jnp.float32).astype(jnp.bfloat16)
    query = query.astype(jnp.float32).reshape(clips, frames, -1, width)
    key = key.astype(jnp.float32).reshape(clips, frames, -1, width)
    value = value.astype(jnp.float32).reshape(clips, frames, -1, width)
    scores = jnp.einsum('cqpd,ckpd->cpqk', query, key) * (1.0 / math.sqrt(width))
    later = jnp.arange(frames)[:, None] >= jnp.arange(frames)[None, :]
    scores = jnp.where(later[None, None], scores, -jnp.inf)
    top_score = lax.optimization_barrier(jnp.max(scores, -1, keepdims=True))
    weights = jnp.exp(scores - top_score)
    totals = lax.optimization_barrier(jnp.sum(weights, -1))
    attended = jnp.einsum('cpqk,ckpd->cqpd', weights, value) / jnp.transpose(totals, (0, 2, 1))[..., None]
    attended = attended.astype(jnp.bfloat16).reshape(-1, width)
    out = jnp.dot(attended, w_out, preferred_element_type=jnp.float32)
    student = (coarse.astype(jnp.float32) + out).astype(jnp.bfloat16)
    diff_top = (student.astype(jnp.float32) - teacher_top.reshape(-1, width).astype(jnp.float32)).astype(jnp.bfloat16)
    scale_top = 1.0 / math.sqrt(attended.shape[0])
    grad_out = jnp.dot(attended.T, diff_top, preferred_element_type=jnp.float32) * scale_top
    return (student.reshape(teacher_top.shape), grad_temporal, grad_out)
```

```python
import functools
import math

import jax
import jax.numpy as jnp
from jax import lax
from jax.experimental import pallas as pl
from jax.experimental.pallas import tpu as pltpu
from jax.sharding import PartitionSpec as P

MESH = pl.DeviceIdType.MESH
F32 = jnp.float32
BF16 = jnp.bfloat16


def dot(a, b):
    return jnp.dot(a, b, preferred_element_type=F32)


def dot_t(a, b):
    return lax.dot_general(a, b, (((0,), (0,)), ((), ())), preferred_element_type=F32)


def kernel(
    frames, spaces, scale_mid, scale_top,
    feats, w_sp, w_tm, teach, w_dn, w_q, w_k, w_v, w_o, teach_top,
    student_out, gt_out, go_out,
    home, v_sp, v_tm, v_dn, v_q, v_k, v_v, v_o,
    cells, edge_send, edges, edge_near, shifted, spat, teacher, teacher_top, mid32, stu,
    in_sem, own_sem, fs, fr, es, er, ts, tr, ps, pr_, ss, sr, hs, hr,
):
    t = lax.axis_index("tm")
    s = lax.axis_index("space")
    rows, _, wc, chan = feats.shape
    half_rows, _, hc, width = teach_top.shape
    peers = [lax.rem(t + i, frames) for i in range(1, frames)]

    loads = [
        pltpu.make_async_copy(src, dst, in_sem.at[i])
        for i, (src, dst) in enumerate(
            ((feats, home), (w_sp, v_sp), (w_tm, v_tm), (w_dn, v_dn),
             (w_q, v_q), (w_k, v_k), (w_v, v_v), (w_o, v_o))
        )
    ]
    for load in loads:
        load.start()
    own = [
        pltpu.make_async_copy(feats.at[:, t], cells.at[pl.ds(1, rows), t], own_sem.at[0]),
        pltpu.make_async_copy(teach.at[:, t], teacher.at[t], own_sem.at[1]),
        pltpu.make_async_copy(teach_top.at[:, t], teacher_top.at[t], own_sem.at[2]),
    ]
    for copy in own:
        copy.start()

    barrier = pltpu.get_barrier_semaphore()
    for u in peers:
        pl.semaphore_signal(barrier, inc=1, device_id={"tm": u}, device_id_type=MESH)

    @pl.when(s > 0)
    def _():
        pl.semaphore_signal(barrier, inc=1, device_id={"space": s - 1}, device_id_type=MESH)

    @pl.when(s < spaces - 1)
    def _():
        pl.semaphore_signal(barrier, inc=1, device_id={"space": s + 1}, device_id_type=MESH)

    loads[0].wait()
    for u in range(frames):
        if u > 0:
            left = home[:, u - 1, wc - 8:, :].astype(F32)[:, 7, :]
        else:
            left = jnp.zeros((rows, chan), F32)
        if u < frames - 1:
            right = home[:, u + 1, :8, :].astype(F32)[:, 0, :]
        else:
            right = jnp.zeros((rows, chan), F32)
        edge_send[u] = jnp.concatenate([left, right], 0).astype(BF16)

    near = (s > 0).astype(jnp.int32) + (s < spaces - 1).astype(jnp.int32)
    pl.semaphore_wait(barrier, near + (frames - 1))

    def send(src, dst, ssem, rsem, u):
        return pltpu.make_async_remote_copy(
            src_ref=src, dst_ref=dst, send_sem=ssem, recv_sem=rsem,
            device_id={"tm": u}, device_id_type=MESH,
        )

    def feats_copy(u, f):
        return send(home.at[:, u], cells.at[pl.ds(1, rows), f], fs.at[u], fr.at[f], u)

    def edge_copy(u, f):
        return send(edge_send.at[u], edges.at[f], es.at[u], er.at[f], u)

    def teach_copy(u, f):
        return send(teach.at[:, u], teacher.at[f], ts.at[u], tr.at[f], u)

    def top_copy(u, f):
        return send(teach_top.at[:, u], teacher_top.at[f], ps.at[u], pr_.at[f], u)

    def student_copy(u, f):
        return send(stu.at[u], student_out.at[:, f], ss.at[u], sr.at[f], u)

    for u in peers:
        edge_copy(u, t).start()
        feats_copy(u, t).start()
    edges[t] = edge_send[t]
    spat[pl.ds(0, 2)] = jnp.zeros((2,) + spat.shape[1:], BF16)

    @pl.when(s == 0)
    def _():
        cells[0] = jnp.zeros(cells.shape[1:], BF16)
        edge_near[0] = jnp.zeros(edges.shape, BF16)

    @pl.when(s == spaces - 1)
    def _():
        cells[rows + 1] = jnp.zeros(cells.shape[1:], BF16)
        edge_near[1] = jnp.zeros(edges.shape, BF16)

    own[0].wait()
    for f in peers:
        edge_copy(f, f).wait_recv()
        feats_copy(f, f).wait_recv()
    for u in peers:
        teach_copy(u, t).start()
    for u in peers:
        top_copy(u, t).start()

    def halo(src, dst, i, j, to):
        return pltpu.make_async_remote_copy(
            src_ref=src, dst_ref=dst, send_sem=hs.at[i], recv_sem=hr.at[j],
            device_id={"space": to}, device_id_type=MESH,
        )

    def up(to):
        return (halo(cells.at[1], cells.at[rows + 1], 0, 0, to),
                halo(edges, edge_near.at[1], 1, 1, to))

    def down(to):
        return (halo(cells.at[rows], cells.at[0], 2, 2, to),
                halo(edges, edge_near.at[0], 3, 3, to))

    @pl.when(s > 0)
    def _():
        for copy in up(s - 1):
            copy.start()

    @pl.when(s < spaces - 1)
    def _():
        for copy in down(s + 1):
            copy.start()

    column = lax.broadcasted_iota(jnp.int32, (frames, wc, chan), 1)

    def shift(row, left, right):
        x = cells[row].astype(F32)
        a = jnp.where(column == 0, left, pltpu.roll(x, 1, 1))
        b = jnp.where(column == wc - 1, right, pltpu.roll(x, wc - 1, 1))
        flat = (frames * wc, chan)
        shifted[row, :, pl.ds(0, chan)] = a.astype(BF16).reshape(flat)
        shifted[row, :, pl.ds(chan, chan)] = cells[row].reshape(flat)
        shifted[row, :, pl.ds(2 * chan, chan)] = b.astype(BF16).reshape(flat)

    def conv(first, count):
        total = None
        for dy in range(3):
            block = shifted[pl.ds(first + dy, count)].reshape(count * frames * wc, 3 * chan)
            term = dot(block, v_sp[dy])
            total = term if total is None else total + term
        out = (total / (1.0 + jnp.exp(-total))).astype(BF16)
        out = out.reshape(count, frames, wc, chan)
        for i in range(count):
            spat[pl.ds(2, frames), first + i] = out[i]

    side = edges[...].astype(F32)
    for r in range(rows):
        shift(r + 1, side[:, r:r + 1, :], side[:, rows + r:rows + r + 1, :])
    loads[1].wait()
    for first in range(1, rows - 1, 2):
        conv(first, 2)

    @pl.when(s < spaces - 1)
    def _():
        for copy in up(s + 1):
            copy.wait_recv()

    @pl.when(s > 0)
    def _():
        for copy in down(s - 1):
            copy.wait_recv()

    side = edge_near[0].astype(F32)
    shift(0, side[:, rows - 1:rows, :], side[:, 2 * rows - 1:2 * rows, :])
    side = edge_near[1].astype(F32)
    shift(rows + 1, side[:, 0:1, :], side[:, rows:rows + 1, :])
    conv(0, 1)
    conv(rows - 1, 1)

    loads[2].wait()
    half = chan // 2
    for f in range(frames):
        total = None
        for k in range(3):
            term = dot(spat[f + k].reshape(rows * wc, chan), v_tm[pl.ds(k * chan, chan), :])
            total = term if total is None else total + term
        base = cells[pl.ds(1, rows), f].astype(F32).reshape(rows * wc, chan)
        mid = (base + total).astype(BF16).astype(F32)
        for h in range(2):
            mid32[h, pl.ds(f * rows * wc, rows * wc), :] = mid[:, h * half:(h + 1) * half]

    loads[3].wait()
    coarse = None
    count = frames * rows * wc // 2
    for b in range(2):
        part = jnp.concatenate(
            [mid32[h, pl.ds(b, count, stride=2), :] for h in range(2)], -1
        ).reshape(frames * half_rows, 2, hc, chan)
        for a in range(2):
            block = part[:, a].reshape(frames * half_rows * hc, chan).astype(BF16)
            term = dot(block, v_dn[a, b])
            coarse = term if coarse is None else coarse + term
    coarse = coarse.astype(BF16)

    for i in range(4, 8):
        loads[i].wait()
    points = half_rows * hc
    query = dot(coarse, v_q[...]).astype(BF16).astype(F32).reshape(frames, points, width)
    key = dot(coarse, v_k[...]).astype(BF16).astype(F32).reshape(frames, points, width)
    value = dot(coarse, v_v[...]).astype(BF16).astype(F32).reshape(frames, points, width)
    scale = 1.0 / math.sqrt(width)
    results = []
    for q in range(frames):
        score = [jnp.sum(query[q] * key[k], -1, keepdims=True) * scale for k in range(q + 1)]
        top = functools.reduce(jnp.maximum, score)
        weight = [jnp.exp(x - top) for x in score]
        total = functools.reduce(jnp.add, weight)
        acc = functools.reduce(jnp.add, [weight[k] * value[k] for k in range(q + 1)])
        results.append(acc / total)
    attended = jnp.concatenate(results, 0).astype(BF16)
    student = (coarse.astype(F32) + dot(attended, v_o[...])).astype(BF16)
    stu[...] = student.reshape(frames, half_rows, hc, width)
    for u in peers:
        student_copy(u, t).start()
    keep = pltpu.make_async_copy(stu.at[t], student_out.at[:, t], own_sem.at[3])
    keep.start()

    own[1].wait()
    for f in peers:
        teach_copy(f, f).wait_recv()
    n = frames * rows * wc
    mid = jnp.concatenate([mid32[0], mid32[1]], -1)
    diff = (mid - teacher[...].astype(F32).reshape(n, chan)).astype(BF16)
    for k in range(3):
        gt_out[pl.ds(k * chan, chan), :] = (
            dot_t(spat[pl.ds(k, frames)].reshape(n, chan), diff) * scale_mid
        )
    own[2].wait()
    for f in peers:
        top_copy(f, f).wait_recv()
    diff_top = (
        student.astype(F32) - teacher_top[...].astype(F32).reshape(frames * points, width)
    ).astype(BF16)
    go_out[...] = dot_t(attended, diff_top) * scale_top

    keep.wait()
    for u in peers:
        student_copy(u, u).wait_recv()
    for u in peers:
        edge_copy(u, t).wait_send()
        feats_copy(u, t).wait_send()
        teach_copy(u, t).wait_send()
        top_copy(u, t).wait_send()
        student_copy(u, t).wait_send()

    @pl.when(s > 0)
    def _():
        for copy in up(s - 1):
            copy.wait_send()

    @pl.when(s < spaces - 1)
    def _():
        for copy in down(s + 1):
            copy.wait_send()


def local(
    feats, w_spatial, w_temporal, teacher_mid, w_down, w_query, w_key, w_value, w_out, teacher_top
):
    frames = lax.axis_size("tm")
    spaces = lax.axis_size("space")
    devices_all = lax.axis_size("dp") * frames * spaces
    rows, cols, chan = feats.shape[2:]
    half_rows, half_cols, width = teacher_top.shape[2:]
    wc, hc = cols // frames, half_cols // frames
    scale_mid = 1.0 / math.sqrt(rows * cols * devices_all)
    scale_top = 1.0 / math.sqrt(half_rows * half_cols * devices_all)
    dma = pltpu.SemaphoreType.DMA
    student, gt, go = pl.pallas_call(
        functools.partial(kernel, frames, spaces, scale_mid, scale_top),
        out_shape=(
            jax.ShapeDtypeStruct((half_rows, frames, hc, width), BF16),
            jax.ShapeDtypeStruct(w_temporal.shape, F32),
            jax.ShapeDtypeStruct(w_out.shape, F32),
        ),
        in_specs=[pl.BlockSpec(memory_space=pl.ANY)] * 10,
        out_specs=(
            pl.BlockSpec(memory_space=pl.ANY),
            pl.BlockSpec(memory_space=pltpu.VMEM),
            pl.BlockSpec(memory_space=pltpu.VMEM),
        ),
        scratch_shapes=[
            pltpu.VMEM((rows, frames, wc, chan), BF16),
            pltpu.VMEM((3, 3 * chan, chan), BF16),
            pltpu.VMEM(w_temporal.shape, BF16),
            pltpu.VMEM(w_down.shape, BF16),
            pltpu.VMEM(w_query.shape, BF16),
            pltpu.VMEM(w_key.shape, BF16),
            pltpu.VMEM(w_value.shape, BF16),
            pltpu.VMEM(w_out.shape, BF16),
            pltpu.VMEM((rows + 2, frames, wc, chan), BF16),
            pltpu.VMEM((frames, 2 * rows, chan), BF16),
            pltpu.VMEM((frames, 2 * rows, chan), BF16),
            pltpu.VMEM((2, frames, 2 * rows, chan), BF16),
            pltpu.VMEM((rows + 2, frames * wc, 3 * chan), BF16),
            pltpu.VMEM((frames + 2, rows, wc, chan), BF16),
            pltpu.VMEM((frames, rows, wc, chan), BF16),
            pltpu.VMEM((frames, half_rows, hc, width), BF16),
            pltpu.VMEM((2, frames * rows * wc, chan // 2), F32),
            pltpu.VMEM((frames, half_rows, hc, width), BF16),
            dma((8,)),
            dma((4,)),
        ]
        + [dma((frames,))] * 10
        + [dma((4,)), dma((4,))],
        compiler_params=pltpu.CompilerParams(
            collective_id=0, has_side_effects=True, vmem_limit_bytes=40 * 1024 * 1024
        ),
    )(
        feats.reshape(rows, frames, wc, chan),
        w_spatial.reshape(3, 3 * chan, chan),
        w_temporal,
        teacher_mid.reshape(rows, frames, wc, chan),
        w_down,
        w_query,
        w_key,
        w_value,
        w_out,
        teacher_top.reshape(half_rows, frames, hc, width),
    )
    share_t = lax.psum_scatter(gt, ("tm", "space"), scatter_dimension=0, tiled=True)
    share_o = lax.psum_scatter(go, ("tm", "space"), scatter_dimension=0, tiled=True)
    grad_t, grad_o = lax.psum((share_t, share_o), "dp")
    return (student.reshape(1, 1, half_rows, half_cols, width), grad_t, grad_o)


def solution(mesh):
    frame = P("dp", "tm", "space", None, None)
    return jax.shard_map(
        local,
        mesh=mesh,
        in_specs=(frame, P(), P(), frame, P(), P(), P(), P(), P(), frame),
        out_specs=(frame, P(("tm", "space"), None), P(("tm", "space"), None)),
        check_vma=False,
    )
```

```python
import functools
import math

import jax
import jax.numpy as jnp
from jax import lax
from jax.experimental import pallas as pl
from jax.experimental.pallas import tpu as pltpu
from jax.sharding import PartitionSpec as P

MESH = pl.DeviceIdType.MESH
F32 = jnp.float32
BF16 = jnp.bfloat16


def dot(a, b):
    return jnp.dot(a, b, preferred_element_type=F32)


def dot_t(a, b):
    return lax.dot_general(a, b, (((0,), (0,)), ((), ())), preferred_element_type=F32)


class Sum:
    def __init__(self, refs, out, grad, d, me, members, others, spaces):
        (self.part, self.in1, self.half, self.in2, self.quarter, self.in3, self.done,
         self.sem12, self.s3, self.r3, self.s4, self.r4) = refs
        self.out, self.grad, self.d, self.me = out, grad, d, me
        self.members, self.others, self.spaces = members, others, spaces

    def copy(self, src, dst, ssem, rsem, to):
        return pltpu.make_async_remote_copy(
            src_ref=src, dst_ref=dst, send_sem=ssem, recv_sem=rsem,
            device_id=to, device_id_type=MESH,
        )

    def one(self):
        low = lax.rem(self.d, 2)
        return self.copy(self.part.at[1 - low], self.in1, self.sem12.at[0], self.sem12.at[1],
                         {"dp": self.d + 1 - 2 * low})

    def two(self):
        high = self.d // 2
        return self.copy(self.half.at[1 - high], self.in2, self.sem12.at[2], self.sem12.at[3],
                         {"dp": self.d + 2 - 4 * high})

    def three(self, g, f):
        return self.copy(self.quarter.at[g], self.in3.at[f], self.s3.at[g], self.r3.at[f],
                         {"tm": g // self.spaces, "space": lax.rem(g, self.spaces)})

    def four(self, c, f):
        return self.copy(self.done.at[f], self.done.at[f], self.s4.at[c], self.r4.at[f],
                         {"dp": c})

    def first(self):
        _, group, rows, cols = self.part.shape
        split = self.grad.astype(BF16).reshape(group, 2, rows, cols)
        for h in range(2):
            self.part[h] = split[:, h]
        self.one().start()

    def second(self):
        self.one().wait_recv()
        total = self.part[lax.rem(self.d, 2)].astype(F32) + self.in1[...].astype(F32)
        cols = self.half.shape[-1]
        for h in range(2):
            self.half[h] = total[..., h * cols:(h + 1) * cols].astype(BF16)
        self.two().start()

    def third(self):
        self.two().wait_recv()
        total = self.half[self.d // 2].astype(F32) + self.in2[...].astype(F32)
        self.quarter[...] = total.astype(BF16)
        for g in self.members:
            self.three(g, self.me).start()
        self.in3[self.me] = self.quarter[self.me]

    def fourth(self):
        for g in self.members:
            self.three(g, g).wait_recv()
        self.done[self.d] = jnp.sum(self.in3[...].astype(F32), 0)
        for c in self.others:
            self.four(c, self.d).start()

    def finish(self):
        for c in self.others:
            self.four(c, c).wait_recv()
        count, rows, cols = self.done.shape
        for c in range(count):
            self.out[pl.ds((c % 2) * rows, rows), pl.ds((c // 2) * cols, cols)] = self.done[c]
        self.one().wait_send()
        self.two().wait_send()
        for g in self.members:
            self.three(g, self.me).wait_send()
        for c in self.others:
            self.four(c, self.d).wait_send()


def sum_scratch(shape, group, clips):
    dma = pltpu.SemaphoreType.DMA
    rows, cols = shape[0] // group // 2, shape[1]
    return [
        pltpu.VMEM((2, group, rows, cols), BF16),
        pltpu.VMEM((group, rows, cols), BF16),
        pltpu.VMEM((2, group, rows, cols // 2), BF16),
        pltpu.VMEM((group, rows, cols // 2), BF16),
        pltpu.VMEM((group, rows, cols // 2), BF16),
        pltpu.VMEM((group, rows, cols // 2), BF16),
        pltpu.VMEM((clips, rows, cols // 2), F32),
        dma((4,)),
        dma((group,)),
        dma((group,)),
        dma((clips,)),
        dma((clips,)),
    ]


def kernel(
    frames, spaces, clips, reduce, scale_mid, scale_top,
    feats, w_sp, w_tm, teach, w_dn, w_q, w_k, w_v, w_o, teach_top,
    student_out, gt_out, go_out,
    home, v_sp, v_tm, v_dn, v_q, v_k, v_v, v_o,
    cells, edge_send, edges, edge_near, shifted, spat, teacher, teacher_top, mid32, stu,
    in_sem, own_sem, fs, fr, es, er, ts, tr, ps, pr_, ss, sr, hs, hr,
    *sums,
):
    t = lax.axis_index("tm")
    s = lax.axis_index("space")
    rows, _, wc, chan = feats.shape
    half_rows, _, hc, width = teach_top.shape
    peers = [lax.rem(t + i, frames) for i in range(1, frames)]
    group = frames * spaces
    me = t * spaces + s
    members = [lax.rem(me + i, group) for i in range(1, group)]
    d = lax.axis_index("dp")
    others = [lax.rem(d + i, clips) for i in range(1, clips)]

    loads = [
        pltpu.make_async_copy(src, dst, in_sem.at[i])
        for i, (src, dst) in enumerate(
            ((feats, home), (w_sp, v_sp), (w_tm, v_tm), (w_dn, v_dn),
             (w_q, v_q), (w_k, v_k), (w_v, v_v), (w_o, v_o))
        )
    ]
    for load in loads:
        load.start()
    own = [
        pltpu.make_async_copy(feats.at[:, t], cells.at[pl.ds(1, rows), t], own_sem.at[0]),
        pltpu.make_async_copy(teach.at[:, t], teacher.at[t], own_sem.at[1]),
        pltpu.make_async_copy(teach_top.at[:, t], teacher_top.at[t], own_sem.at[2]),
    ]
    for copy in own:
        copy.start()

    barrier = pltpu.get_barrier_semaphore()
    for g in members:
        pl.semaphore_signal(
            barrier, inc=1, device_id={"tm": g // spaces, "space": lax.rem(g, spaces)},
            device_id_type=MESH,
        )
    if reduce:
        for c in others:
            pl.semaphore_signal(barrier, inc=1, device_id={"dp": c}, device_id_type=MESH)

    loads[0].wait()
    for u in range(frames):
        if u > 0:
            left = home[:, u - 1, wc - 8:, :].astype(F32)[:, 7, :]
        else:
            left = jnp.zeros((rows, chan), F32)
        if u < frames - 1:
            right = home[:, u + 1, :8, :].astype(F32)[:, 0, :]
        else:
            right = jnp.zeros((rows, chan), F32)
        edge_send[u] = jnp.concatenate([left, right], 0).astype(BF16)

    pl.semaphore_wait(barrier, group - 1 + (clips - 1 if reduce else 0))

    def send(src, dst, ssem, rsem, u):
        return pltpu.make_async_remote_copy(
            src_ref=src, dst_ref=dst, send_sem=ssem, recv_sem=rsem,
            device_id={"tm": u}, device_id_type=MESH,
        )

    def feats_copy(u, f):
        return send(home.at[:, u], cells.at[pl.ds(1, rows), f], fs.at[u], fr.at[f], u)

    def edge_copy(u, f):
        return send(edge_send.at[u], edges.at[f], es.at[u], er.at[f], u)

    def teach_copy(u, f):
        return send(teach.at[:, u], teacher.at[f], ts.at[u], tr.at[f], u)

    def top_copy(u, f):
        return send(teach_top.at[:, u], teacher_top.at[f], ps.at[u], pr_.at[f], u)

    def student_copy(u, f):
        return send(stu.at[u], student_out.at[:, f], ss.at[u], sr.at[f], u)

    for u in peers:
        edge_copy(u, t).start()
        feats_copy(u, t).start()
    edges[t] = edge_send[t]
    spat[pl.ds(0, 2)] = jnp.zeros((2,) + spat.shape[1:], BF16)

    @pl.when(s == 0)
    def _():
        cells[0] = jnp.zeros(cells.shape[1:], BF16)
        edge_near[0] = jnp.zeros(edges.shape, BF16)

    @pl.when(s == spaces - 1)
    def _():
        cells[rows + 1] = jnp.zeros(cells.shape[1:], BF16)
        edge_near[1] = jnp.zeros(edges.shape, BF16)

    own[0].wait()
    for f in peers:
        edge_copy(f, f).wait_recv()
        feats_copy(f, f).wait_recv()
    for u in peers:
        teach_copy(u, t).start()
    for u in peers:
        top_copy(u, t).start()

    def halo(src, dst, i, j, to):
        return pltpu.make_async_remote_copy(
            src_ref=src, dst_ref=dst, send_sem=hs.at[i], recv_sem=hr.at[j],
            device_id={"space": to}, device_id_type=MESH,
        )

    def up(to):
        return (halo(cells.at[1], cells.at[rows + 1], 0, 0, to),
                halo(edges, edge_near.at[1], 1, 1, to))

    def down(to):
        return (halo(cells.at[rows], cells.at[0], 2, 2, to),
                halo(edges, edge_near.at[0], 3, 3, to))

    @pl.when(s > 0)
    def _():
        for copy in up(s - 1):
            copy.start()

    @pl.when(s < spaces - 1)
    def _():
        for copy in down(s + 1):
            copy.start()

    column = lax.broadcasted_iota(jnp.int32, (frames, wc, chan), 1)

    def shift(row, left, right):
        x = cells[row].astype(F32)
        a = jnp.where(column == 0, left, pltpu.roll(x, 1, 1))
        b = jnp.where(column == wc - 1, right, pltpu.roll(x, wc - 1, 1))
        flat = (frames * wc, chan)
        shifted[row, :, pl.ds(0, chan)] = a.astype(BF16).reshape(flat)
        shifted[row, :, pl.ds(chan, chan)] = cells[row].reshape(flat)
        shifted[row, :, pl.ds(2 * chan, chan)] = b.astype(BF16).reshape(flat)

    def conv(first, count):
        total = None
        for dy in range(3):
            block = shifted[pl.ds(first + dy, count)].reshape(count * frames * wc, 3 * chan)
            term = dot(block, v_sp[dy])
            total = term if total is None else total + term
        out = (total / (1.0 + jnp.exp(-total))).astype(BF16)
        out = out.reshape(count, frames, wc, chan)
        for i in range(count):
            spat[pl.ds(2, frames), first + i] = out[i]

    side = edges[...].astype(F32)
    for r in range(rows):
        shift(r + 1, side[:, r:r + 1, :], side[:, rows + r:rows + r + 1, :])
    loads[1].wait()
    for first in range(1, rows - 1, 2):
        conv(first, 2)

    @pl.when(s < spaces - 1)
    def _():
        for copy in up(s + 1):
            copy.wait_recv()

    @pl.when(s > 0)
    def _():
        for copy in down(s - 1):
            copy.wait_recv()

    side = edge_near[0].astype(F32)
    shift(0, side[:, rows - 1:rows, :], side[:, 2 * rows - 1:2 * rows, :])
    side = edge_near[1].astype(F32)
    shift(rows + 1, side[:, 0:1, :], side[:, rows:rows + 1, :])
    conv(0, 1)
    conv(rows - 1, 1)

    loads[2].wait()
    half = chan // 2
    for f in range(frames):
        total = None
        for k in range(3):
            term = dot(spat[f + k].reshape(rows * wc, chan), v_tm[pl.ds(k * chan, chan), :])
            total = term if total is None else total + term
        base = cells[pl.ds(1, rows), f].astype(F32).reshape(rows * wc, chan)
        mid = (base + total).astype(BF16).astype(F32)
        for h in range(2):
            mid32[h, pl.ds(f * rows * wc, rows * wc), :] = mid[:, h * half:(h + 1) * half]

    loads[3].wait()
    coarse = None
    count = frames * rows * wc // 2
    for b in range(2):
        part = jnp.concatenate(
            [mid32[h, pl.ds(b, count, stride=2), :] for h in range(2)], -1
        ).reshape(frames * half_rows, 2, hc, chan)
        for a in range(2):
            block = part[:, a].reshape(frames * half_rows * hc, chan).astype(BF16)
            term = dot(block, v_dn[a, b])
            coarse = term if coarse is None else coarse + term
    coarse = coarse.astype(BF16)

    for i in range(4, 8):
        loads[i].wait()
    points = half_rows * hc
    query = dot(coarse, v_q[...]).astype(BF16).astype(F32).reshape(frames, points, width)
    key = dot(coarse, v_k[...]).astype(BF16).astype(F32).reshape(frames, points, width)
    value = dot(coarse, v_v[...]).astype(BF16).astype(F32).reshape(frames, points, width)
    scale = 1.0 / math.sqrt(width)
    results = []
    for q in range(frames):
        score = [jnp.sum(query[q] * key[k], -1, keepdims=True) * scale for k in range(q + 1)]
        top = functools.reduce(jnp.maximum, score)
        weight = [jnp.exp(x - top) for x in score]
        total = functools.reduce(jnp.add, weight)
        acc = functools.reduce(jnp.add, [weight[k] * value[k] for k in range(q + 1)])
        results.append(acc / total)
    attended = jnp.concatenate(results, 0).astype(BF16)
    student = (coarse.astype(F32) + dot(attended, v_o[...])).astype(BF16)
    stu[...] = student.reshape(frames, half_rows, hc, width)
    for u in peers:
        student_copy(u, t).start()
    keep = pltpu.make_async_copy(stu.at[t], student_out.at[:, t], own_sem.at[3])
    keep.start()

    own[1].wait()
    for f in peers:
        teach_copy(f, f).wait_recv()
    n = frames * rows * wc
    mid = jnp.concatenate([mid32[0], mid32[1]], -1)
    diff = (mid - teacher[...].astype(F32).reshape(n, chan)).astype(BF16)
    grad = jnp.concatenate(
        [dot_t(spat[pl.ds(k, frames)].reshape(n, chan), diff) * scale_mid for k in range(3)], 0
    )
    if reduce:
        mid_sum = Sum(sums[:12], gt_out, grad, d, me, members, others, spaces)
        mid_sum.first()
    else:
        gt_out[...] = grad
    own[2].wait()
    for f in peers:
        top_copy(f, f).wait_recv()
    diff_top = (
        student.astype(F32) - teacher_top[...].astype(F32).reshape(frames * points, width)
    ).astype(BF16)
    grad = dot_t(attended, diff_top) * scale_top
    if reduce:
        top_sum = Sum(sums[12:], go_out, grad, d, me, members, others, spaces)
        top_sum.first()
        mid_sum.second()
        top_sum.second()
        mid_sum.third()
        top_sum.third()
        mid_sum.fourth()
        top_sum.fourth()
        mid_sum.finish()
        top_sum.finish()
    else:
        go_out[...] = grad

    keep.wait()
    for u in peers:
        student_copy(u, u).wait_recv()
    for u in peers:
        edge_copy(u, t).wait_send()
        feats_copy(u, t).wait_send()
        teach_copy(u, t).wait_send()
        top_copy(u, t).wait_send()
        student_copy(u, t).wait_send()

    @pl.when(s > 0)
    def _():
        for copy in up(s - 1):
            copy.wait_send()

    @pl.when(s < spaces - 1)
    def _():
        for copy in down(s + 1):
            copy.wait_send()


def local(
    feats, w_spatial, w_temporal, teacher_mid, w_down, w_query, w_key, w_value, w_out, teacher_top
):
    frames = lax.axis_size("tm")
    spaces = lax.axis_size("space")
    devices_all = lax.axis_size("dp") * frames * spaces
    rows, cols, chan = feats.shape[2:]
    half_rows, half_cols, width = teacher_top.shape[2:]
    wc, hc = cols // frames, half_cols // frames
    scale_mid = 1.0 / math.sqrt(rows * cols * devices_all)
    scale_top = 1.0 / math.sqrt(half_rows * half_cols * devices_all)
    dma = pltpu.SemaphoreType.DMA
    group, clips = frames * spaces, lax.axis_size("dp")
    grads = (w_temporal.shape, w_out.shape)
    reduce = clips == 4 and all(r % (32 * group) == 0 and c % 256 == 0 for r, c in grads)
    pieces = [(r // group, c) if reduce else (r, c) for r, c in grads]
    student, gt, go = pl.pallas_call(
        functools.partial(kernel, frames, spaces, clips, reduce, scale_mid, scale_top),
        out_shape=(
            jax.ShapeDtypeStruct((half_rows, frames, hc, width), BF16),
            jax.ShapeDtypeStruct(pieces[0], F32),
            jax.ShapeDtypeStruct(pieces[1], F32),
        ),
        in_specs=[pl.BlockSpec(memory_space=pl.ANY)] * 10,
        out_specs=(
            pl.BlockSpec(memory_space=pl.ANY),
            pl.BlockSpec(memory_space=pltpu.VMEM),
            pl.BlockSpec(memory_space=pltpu.VMEM),
        ),
        scratch_shapes=[
            pltpu.VMEM((rows, frames, wc, chan), BF16),
            pltpu.VMEM((3, 3 * chan, chan), BF16),
            pltpu.VMEM(w_temporal.shape, BF16),
            pltpu.VMEM(w_down.shape, BF16),
            pltpu.VMEM(w_query.shape, BF16),
            pltpu.VMEM(w_key.shape, BF16),
            pltpu.VMEM(w_value.shape, BF16),
            pltpu.VMEM(w_out.shape, BF16),
            pltpu.VMEM((rows + 2, frames, wc, chan), BF16),
            pltpu.VMEM((frames, 2 * rows, chan), BF16),
            pltpu.VMEM((frames, 2 * rows, chan), BF16),
            pltpu.VMEM((2, frames, 2 * rows, chan), BF16),
            pltpu.VMEM((rows + 2, frames * wc, 3 * chan), BF16),
            pltpu.VMEM((frames + 2, rows, wc, chan), BF16),
            pltpu.VMEM((frames, rows, wc, chan), BF16),
            pltpu.VMEM((frames, half_rows, hc, width), BF16),
            pltpu.VMEM((2, frames * rows * wc, chan // 2), F32),
            pltpu.VMEM((frames, half_rows, hc, width), BF16),
            dma((8,)),
            dma((4,)),
        ]
        + [dma((frames,))] * 10
        + [dma((4,)), dma((4,))]
        + (sum_scratch(grads[0], group, clips) + sum_scratch(grads[1], group, clips) if reduce else []),
        compiler_params=pltpu.CompilerParams(
            collective_id=0, has_side_effects=True, vmem_limit_bytes=58 * 1024 * 1024
        ),
    )(
        feats.reshape(rows, frames, wc, chan),
        w_spatial.reshape(3, 3 * chan, chan),
        w_temporal,
        teacher_mid.reshape(rows, frames, wc, chan),
        w_down,
        w_query,
        w_key,
        w_value,
        w_out,
        teacher_top.reshape(half_rows, frames, hc, width),
    )
    if not reduce:
        gt = lax.psum_scatter(gt, ("tm", "space"), scatter_dimension=0, tiled=True)
        go = lax.psum_scatter(go, ("tm", "space"), scatter_dimension=0, tiled=True)
        gt, go = lax.psum((gt, go), "dp")
    return (student.reshape(1, 1, half_rows, half_cols, width), gt, go)


def solution(mesh):
    frame = P("dp", "tm", "space", None, None)
    return jax.shard_map(
        local,
        mesh=mesh,
        in_specs=(frame, P(), P(), frame, P(), P(), P(), P(), P(), frame),
        out_specs=(frame, P(("tm", "space"), None), P(("tm", "space"), None)),
        check_vma=False,
    )
```

```python
import functools
import math

import jax
import jax.numpy as jnp
from jax import lax
from jax.experimental import pallas as pl
from jax.experimental.pallas import tpu as pltpu
from jax.sharding import PartitionSpec as P

MESH = pl.DeviceIdType.MESH
F32 = jnp.float32
BF16 = jnp.bfloat16


def dot(a, b):
    return jnp.dot(a, b, preferred_element_type=F32)


def dot_t(a, b):
    return lax.dot_general(a, b, (((0,), (0,)), ((), ())), preferred_element_type=F32)


class Sum:
    def __init__(self, refs, out, grad, d, me, members, others, spaces):
        (self.part, self.in1, self.half, self.in2, self.quarter, self.in3, self.done,
         self.sem12, self.s3, self.r3, self.s4, self.r4) = refs
        self.out, self.grad, self.d, self.me = out, grad, d, me
        self.members, self.others, self.spaces = members, others, spaces

    def copy(self, src, dst, ssem, rsem, to):
        return pltpu.make_async_remote_copy(
            src_ref=src, dst_ref=dst, send_sem=ssem, recv_sem=rsem,
            device_id=to, device_id_type=MESH,
        )

    def one(self):
        low = lax.rem(self.d, 2)
        return self.copy(self.part.at[1 - low], self.in1, self.sem12.at[0], self.sem12.at[1],
                         {"dp": self.d + 1 - 2 * low})

    def two(self):
        high = self.d // 2
        return self.copy(self.half.at[1 - high], self.in2, self.sem12.at[2], self.sem12.at[3],
                         {"dp": self.d + 2 - 4 * high})

    def three(self, g, f):
        return self.copy(self.quarter.at[g], self.in3.at[f], self.s3.at[g], self.r3.at[f],
                         {"tm": g // self.spaces, "space": lax.rem(g, self.spaces)})

    def four(self, c, f):
        return self.copy(self.done.at[f], self.done.at[f], self.s4.at[c], self.r4.at[f],
                         {"dp": c})

    def first(self):
        _, group, rows, cols = self.part.shape
        split = self.grad.astype(BF16).reshape(group, 2, rows, cols)
        for h in range(2):
            self.part[h] = split[:, h]
        self.one().start()

    def second(self):
        self.one().wait_recv()
        total = self.part[lax.rem(self.d, 2)].astype(F32) + self.in1[...].astype(F32)
        cols = self.half.shape[-1]
        for h in range(2):
            self.half[h] = total[..., h * cols:(h + 1) * cols].astype(BF16)
        self.two().start()

    def third(self):
        self.two().wait_recv()
        total = self.half[self.d // 2].astype(F32) + self.in2[...].astype(F32)
        self.quarter[...] = total.astype(BF16)
        for g in self.members:
            self.three(g, self.me).start()
        self.in3[self.me] = self.quarter[self.me]

    def fourth(self):
        for g in self.members:
            self.three(g, g).wait_recv()
        self.done[self.d] = jnp.sum(self.in3[...].astype(F32), 0).astype(BF16)
        for c in self.others:
            self.four(c, self.d).start()

    def finish(self):
        for c in self.others:
            self.four(c, c).wait_recv()
        count, rows, cols = self.done.shape
        for c in range(count):
            self.out[pl.ds((c % 2) * rows, rows), pl.ds((c // 2) * cols, cols)] = self.done[c].astype(F32)
        self.one().wait_send()
        self.two().wait_send()
        for g in self.members:
            self.three(g, self.me).wait_send()
        for c in self.others:
            self.four(c, self.d).wait_send()


def sum_scratch(shape, group, clips):
    dma = pltpu.SemaphoreType.DMA
    rows, cols = shape[0] // group // 2, shape[1]
    return [
        pltpu.VMEM((2, group, rows, cols), BF16),
        pltpu.VMEM((group, rows, cols), BF16),
        pltpu.VMEM((2, group, rows, cols // 2), BF16),
        pltpu.VMEM((group, rows, cols // 2), BF16),
        pltpu.VMEM((group, rows, cols // 2), BF16),
        pltpu.VMEM((group, rows, cols // 2), BF16),
        pltpu.VMEM((clips, rows, cols // 2), BF16),
        dma((4,)),
        dma((group,)),
        dma((group,)),
        dma((clips,)),
        dma((clips,)),
    ]


def kernel(
    frames, spaces, clips, reduce, scale_mid, scale_top,
    feats, w_sp, w_tm, teach, w_dn, w_q, w_k, w_v, w_o, teach_top,
    student_out, gt_out, go_out,
    home, v_sp, v_tm, v_dn, v_q, v_k, v_v, v_o,
    cells, edge_send, edges, edge_near, shifted, spat, teacher, teacher_top, mid32, stu,
    in_sem, own_sem, fs, fr, es, er, ts, tr, ps, pr_, ss, sr, hs, hr,
    *sums,
):
    t = lax.axis_index("tm")
    s = lax.axis_index("space")
    rows, _, wc, chan = feats.shape
    half_rows, _, hc, width = teach_top.shape
    peers = [lax.rem(t + i, frames) for i in range(1, frames)]
    group = frames * spaces
    me = t * spaces + s
    members = [lax.rem(me + i, group) for i in range(1, group)]
    d = lax.axis_index("dp")
    others = [lax.rem(d + i, clips) for i in range(1, clips)]

    loads = [
        pltpu.make_async_copy(src, dst, in_sem.at[i])
        for i, (src, dst) in enumerate(
            ((feats, home), (w_sp, v_sp), (w_tm, v_tm), (w_dn, v_dn),
             (w_q, v_q), (w_k, v_k), (w_v, v_v), (w_o, v_o))
        )
    ]
    for load in loads:
        load.start()
    own = [
        pltpu.make_async_copy(feats.at[:, t], cells.at[pl.ds(1, rows), t], own_sem.at[0]),
        pltpu.make_async_copy(teach.at[:, t], teacher.at[t], own_sem.at[1]),
        pltpu.make_async_copy(teach_top.at[:, t], teacher_top.at[t], own_sem.at[2]),
    ]
    for copy in own:
        copy.start()

    barrier = pltpu.get_barrier_semaphore()
    for g in members:
        pl.semaphore_signal(
            barrier, inc=1, device_id={"tm": g // spaces, "space": lax.rem(g, spaces)},
            device_id_type=MESH,
        )
    if reduce:
        for c in others:
            pl.semaphore_signal(barrier, inc=1, device_id={"dp": c}, device_id_type=MESH)

    loads[0].wait()
    for u in range(frames):
        if u > 0:
            left = home[:, u - 1, wc - 8:, :].astype(F32)[:, 7, :]
        else:
            left = jnp.zeros((rows, chan), F32)
        if u < frames - 1:
            right = home[:, u + 1, :8, :].astype(F32)[:, 0, :]
        else:
            right = jnp.zeros((rows, chan), F32)
        edge_send[u] = jnp.concatenate([left, right], 0).astype(BF16)

    pl.semaphore_wait(barrier, group - 1 + (clips - 1 if reduce else 0))

    def send(src, dst, ssem, rsem, u):
        return pltpu.make_async_remote_copy(
            src_ref=src, dst_ref=dst, send_sem=ssem, recv_sem=rsem,
            device_id={"tm": u}, device_id_type=MESH,
        )

    def feats_copy(u, f):
        return send(home.at[:, u], cells.at[pl.ds(1, rows), f], fs.at[u], fr.at[f], u)

    def edge_copy(u, f):
        return send(edge_send.at[u], edges.at[f], es.at[u], er.at[f], u)

    def teach_copy(u, f):
        return send(teach.at[:, u], teacher.at[f], ts.at[u], tr.at[f], u)

    def top_copy(u, f):
        return send(teach_top.at[:, u], teacher_top.at[f], ps.at[u], pr_.at[f], u)

    def student_copy(u, f):
        return send(stu.at[u], student_out.at[:, f], ss.at[u], sr.at[f], u)

    for u in peers:
        edge_copy(u, t).start()
        feats_copy(u, t).start()
    edges[t] = edge_send[t]
    spat[pl.ds(0, 2)] = jnp.zeros((2,) + spat.shape[1:], BF16)

    @pl.when(s == 0)
    def _():
        cells[0] = jnp.zeros(cells.shape[1:], BF16)
        edge_near[0] = jnp.zeros(edges.shape, BF16)

    @pl.when(s == spaces - 1)
    def _():
        cells[rows + 1] = jnp.zeros(cells.shape[1:], BF16)
        edge_near[1] = jnp.zeros(edges.shape, BF16)

    own[0].wait()
    for f in peers:
        edge_copy(f, f).wait_recv()
        feats_copy(f, f).wait_recv()
    for u in peers:
        teach_copy(u, t).start()

    def halo(src, dst, i, j, to):
        return pltpu.make_async_remote_copy(
            src_ref=src, dst_ref=dst, send_sem=hs.at[i], recv_sem=hr.at[j],
            device_id={"space": to}, device_id_type=MESH,
        )

    def up(to):
        return (halo(cells.at[1], cells.at[rows + 1], 0, 0, to),
                halo(edges, edge_near.at[1], 1, 1, to))

    def down(to):
        return (halo(cells.at[rows], cells.at[0], 2, 2, to),
                halo(edges, edge_near.at[0], 3, 3, to))

    @pl.when(s > 0)
    def _():
        for copy in up(s - 1):
            copy.start()

    @pl.when(s < spaces - 1)
    def _():
        for copy in down(s + 1):
            copy.start()

    column = lax.broadcasted_iota(jnp.int32, (frames, wc, chan), 1)

    def shift(row, left, right):
        x = cells[row].astype(F32)
        a = jnp.where(column == 0, left, pltpu.roll(x, 1, 1))
        b = jnp.where(column == wc - 1, right, pltpu.roll(x, wc - 1, 1))
        flat = (frames * wc, chan)
        shifted[row, :, pl.ds(0, chan)] = a.astype(BF16).reshape(flat)
        shifted[row, :, pl.ds(chan, chan)] = cells[row].reshape(flat)
        shifted[row, :, pl.ds(2 * chan, chan)] = b.astype(BF16).reshape(flat)

    def conv(first, count):
        total = None
        for dy in range(3):
            block = shifted[pl.ds(first + dy, count)].reshape(count * frames * wc, 3 * chan)
            term = dot(block, v_sp[dy])
            total = term if total is None else total + term
        out = (total / (1.0 + jnp.exp(-total))).astype(BF16)
        out = out.reshape(count, frames, wc, chan)
        for i in range(count):
            spat[pl.ds(2, frames), first + i] = out[i]

    side = edges[...].astype(F32)
    for r in range(rows):
        shift(r + 1, side[:, r:r + 1, :], side[:, rows + r:rows + r + 1, :])
    loads[1].wait()
    conv(1, rows - 2)

    @pl.when(s < spaces - 1)
    def _():
        for copy in up(s + 1):
            copy.wait_recv()

    @pl.when(s > 0)
    def _():
        for copy in down(s - 1):
            copy.wait_recv()

    side = edge_near[0].astype(F32)
    shift(0, side[:, rows - 1:rows, :], side[:, 2 * rows - 1:2 * rows, :])
    side = edge_near[1].astype(F32)
    shift(rows + 1, side[:, 0:1, :], side[:, rows:rows + 1, :])
    conv(0, 1)
    conv(rows - 1, 1)

    loads[2].wait()
    half = chan // 2
    n = frames * rows * wc
    total = None
    for k in range(3):
        term = dot(spat[pl.ds(k, frames)].reshape(n, chan), v_tm[pl.ds(k * chan, chan), :])
        total = term if total is None else total + term
    for f in range(frames):
        base = cells[pl.ds(1, rows), f].astype(F32).reshape(rows * wc, chan)
        span = slice(f * rows * wc, (f + 1) * rows * wc)
        mid = (base + total[span]).astype(BF16).astype(F32)
        for h in range(2):
            mid32[h, span, :] = mid[:, h * half:(h + 1) * half]

    loads[3].wait()
    coarse = None
    count = frames * rows * wc // 2
    for b in range(2):
        part = jnp.concatenate(
            [mid32[h, pl.ds(b, count, stride=2), :] for h in range(2)], -1
        ).reshape(frames * half_rows, 2, hc, chan)
        for a in range(2):
            block = part[:, a].reshape(frames * half_rows * hc, chan).astype(BF16)
            term = dot(block, v_dn[a, b])
            coarse = term if coarse is None else coarse + term
    coarse = coarse.astype(BF16)

    for i in range(4, 8):
        loads[i].wait()
    points = half_rows * hc
    query = dot(coarse, v_q[...]).astype(BF16).astype(F32).reshape(frames, points, width)
    key = dot(coarse, v_k[...]).astype(BF16).astype(F32).reshape(frames, points, width)
    value = dot(coarse, v_v[...]).astype(BF16).astype(F32).reshape(frames, points, width)
    scale = 1.0 / math.sqrt(width)
    results = []
    for q in range(frames):
        score = [jnp.sum(query[q] * key[k], -1, keepdims=True) * scale for k in range(q + 1)]
        top = functools.reduce(jnp.maximum, score)
        weight = [jnp.exp(x - top) for x in score]
        total = functools.reduce(jnp.add, weight)
        acc = functools.reduce(jnp.add, [weight[k] * value[k] for k in range(q + 1)])
        results.append(acc / total)
    attended = jnp.concatenate(results, 0).astype(BF16)
    student = (coarse.astype(F32) + dot(attended, v_o[...])).astype(BF16)
    stu[...] = student.reshape(frames, half_rows, hc, width)
    keep = pltpu.make_async_copy(stu.at[t], student_out.at[:, t], own_sem.at[3])
    keep.start()

    own[1].wait()
    for f in peers:
        teach_copy(f, f).wait_recv()
    for u in peers:
        top_copy(u, t).start()
    mid = jnp.concatenate([mid32[0], mid32[1]], -1)
    diff = (mid - teacher[...].astype(F32).reshape(n, chan)).astype(BF16)
    grad = jnp.concatenate(
        [dot_t(spat[pl.ds(k, frames)].reshape(n, chan), diff) * scale_mid for k in range(3)], 0
    )
    if reduce:
        mid_sum = Sum(sums[:12], gt_out, grad, d, me, members, others, spaces)
        mid_sum.first()
    else:
        gt_out[...] = grad
    own[2].wait()
    for f in peers:
        top_copy(f, f).wait_recv()
    for u in peers:
        student_copy(u, t).start()
    diff_top = (
        student.astype(F32) - teacher_top[...].astype(F32).reshape(frames * points, width)
    ).astype(BF16)
    grad = dot_t(attended, diff_top) * scale_top
    if reduce:
        top_sum = Sum(sums[12:], go_out, grad, d, me, members, others, spaces)
        top_sum.first()
        mid_sum.second()
        top_sum.second()
        mid_sum.third()
        top_sum.third()
        mid_sum.fourth()
        top_sum.fourth()
        mid_sum.finish()
        top_sum.finish()
    else:
        go_out[...] = grad

    keep.wait()
    for u in peers:
        student_copy(u, u).wait_recv()
    for u in peers:
        edge_copy(u, t).wait_send()
        feats_copy(u, t).wait_send()
        teach_copy(u, t).wait_send()
        top_copy(u, t).wait_send()
        student_copy(u, t).wait_send()

    @pl.when(s > 0)
    def _():
        for copy in up(s - 1):
            copy.wait_send()

    @pl.when(s < spaces - 1)
    def _():
        for copy in down(s + 1):
            copy.wait_send()


def hand_over(*refs):
    count = len(refs) // 2
    sems = refs[-1]
    copies = [
        pltpu.make_async_copy(refs[i], refs[count + i], sems.at[i]) for i in range(count)
    ]
    for copy in copies:
        copy.start()
    for copy in copies:
        copy.wait()


def local(
    feats, w_spatial, w_temporal, teacher_mid, w_down, w_query, w_key, w_value, w_out, teacher_top
):
    frames = lax.axis_size("tm")
    spaces = lax.axis_size("space")
    devices_all = lax.axis_size("dp") * frames * spaces
    rows, cols, chan = feats.shape[2:]
    half_rows, half_cols, width = teacher_top.shape[2:]
    wc, hc = cols // frames, half_cols // frames
    scale_mid = 1.0 / math.sqrt(rows * cols * devices_all)
    scale_top = 1.0 / math.sqrt(half_rows * half_cols * devices_all)
    dma = pltpu.SemaphoreType.DMA
    group, clips = frames * spaces, lax.axis_size("dp")
    grads = (w_temporal.shape, w_out.shape)
    reduce = clips == 4 and all(r % (32 * group) == 0 and c % 256 == 0 for r, c in grads)
    pieces = [(r // group, c) if reduce else (r, c) for r, c in grads]
    student, gt, go = pl.pallas_call(
        functools.partial(kernel, frames, spaces, clips, reduce, scale_mid, scale_top),
        out_shape=(
            jax.ShapeDtypeStruct((half_rows, frames, hc, width), BF16),
            jax.ShapeDtypeStruct(pieces[0], F32),
            jax.ShapeDtypeStruct(pieces[1], F32),
        ),
        in_specs=[pl.BlockSpec(memory_space=pl.ANY)] * 10,
        out_specs=(
            pl.BlockSpec(memory_space=pl.ANY),
            pl.BlockSpec(memory_space=pltpu.VMEM),
            pl.BlockSpec(memory_space=pltpu.VMEM),
        ),
        scratch_shapes=[
            pltpu.VMEM((rows, frames, wc, chan), BF16),
            pltpu.VMEM((3, 3 * chan, chan), BF16),
            pltpu.VMEM(w_temporal.shape, BF16),
            pltpu.VMEM(w_down.shape, BF16),
            pltpu.VMEM(w_query.shape, BF16),
            pltpu.VMEM(w_key.shape, BF16),
            pltpu.VMEM(w_value.shape, BF16),
            pltpu.VMEM(w_out.shape, BF16),
            pltpu.VMEM((rows + 2, frames, wc, chan), BF16),
            pltpu.VMEM((frames, 2 * rows, chan), BF16),
            pltpu.VMEM((frames, 2 * rows, chan), BF16),
            pltpu.VMEM((2, frames, 2 * rows, chan), BF16),
            pltpu.VMEM((rows + 2, frames * wc, 3 * chan), BF16),
            pltpu.VMEM((frames + 2, rows, wc, chan), BF16),
            pltpu.VMEM((frames, rows, wc, chan), BF16),
            pltpu.VMEM((frames, half_rows, hc, width), BF16),
            pltpu.VMEM((2, frames * rows * wc, chan // 2), F32),
            pltpu.VMEM((frames, half_rows, hc, width), BF16),
            dma((8,)),
            dma((4,)),
        ]
        + [dma((frames,))] * 10
        + [dma((4,)), dma((4,))]
        + (sum_scratch(grads[0], group, clips) + sum_scratch(grads[1], group, clips) if reduce else []),
        compiler_params=pltpu.CompilerParams(
            collective_id=0, has_side_effects=True, vmem_limit_bytes=58 * 1024 * 1024
        ),
    )(
        feats.reshape(rows, frames, wc, chan),
        w_spatial.reshape(3, 3 * chan, chan),
        w_temporal,
        teacher_mid.reshape(rows, frames, wc, chan),
        w_down,
        w_query,
        w_key,
        w_value,
        w_out,
        teacher_top.reshape(half_rows, frames, hc, width),
    )
    if reduce:
        student, gt, go = pl.pallas_call(
            hand_over,
            out_shape=tuple(jax.ShapeDtypeStruct(x.shape, x.dtype) for x in (student, gt, go)),
            in_specs=[pl.BlockSpec(memory_space=pl.ANY)] * 3,
            out_specs=(pl.BlockSpec(memory_space=pl.ANY),) * 3,
            scratch_shapes=[dma((3,))],
            compiler_params=pltpu.CompilerParams(vmem_limit_bytes=58 * 1024 * 1024),
        )(student, gt, go)
    else:
        gt = lax.psum_scatter(gt, ("tm", "space"), scatter_dimension=0, tiled=True)
        go = lax.psum_scatter(go, ("tm", "space"), scatter_dimension=0, tiled=True)
        gt, go = lax.psum((gt, go), "dp")
    return (student.reshape(1, 1, half_rows, half_cols, width), gt, go)


def solution(mesh):
    frame = P("dp", "tm", "space", None, None)
    return jax.shard_map(
        local,
        mesh=mesh,
        in_specs=(frame, P(), P(), frame, P(), P(), P(), P(), P(), frame),
        out_specs=(frame, P(("tm", "space"), None), P(("tm", "space"), None)),
        check_vma=False,
    )
```

```python
import functools
import math

import jax
import jax.numpy as jnp
from jax import lax
from jax.experimental import pallas as pl
from jax.experimental.pallas import tpu as pltpu
from jax.sharding import PartitionSpec as P

MESH = pl.DeviceIdType.MESH
F32 = jnp.float32
BF16 = jnp.bfloat16


def dot(a, b):
    return jnp.dot(a, b, preferred_element_type=F32)


class Sum:
    def __init__(self, refs, out, grad, d, me, members, others, spaces):
        (self.part, self.in1, self.half, self.in2, self.quarter, self.in3, self.done,
         self.sem12, self.s3, self.r3, self.s4, self.r4) = refs
        self.out, self.grad, self.d, self.me = out, grad, d, me
        self.members, self.others, self.spaces = members, others, spaces

    def copy(self, src, dst, ssem, rsem, to):
        return pltpu.make_async_remote_copy(
            src_ref=src, dst_ref=dst, send_sem=ssem, recv_sem=rsem,
            device_id=to, device_id_type=MESH,
        )

    def one(self):
        low = lax.rem(self.d, 2)
        return self.copy(self.part.at[1 - low], self.in1, self.sem12.at[0], self.sem12.at[1],
                         {"dp": self.d + 1 - 2 * low})

    def two(self):
        high = self.d // 2
        return self.copy(self.half.at[1 - high], self.in2, self.sem12.at[2], self.sem12.at[3],
                         {"dp": self.d + 2 - 4 * high})

    def three(self, g, f):
        return self.copy(self.quarter.at[g], self.in3.at[f], self.s3.at[g], self.r3.at[f],
                         {"tm": g // self.spaces, "space": lax.rem(g, self.spaces)})

    def four(self, c, f):
        return self.copy(self.done.at[f], self.done.at[f], self.s4.at[c], self.r4.at[f],
                         {"dp": c})

    def first(self):
        _, group, rows, cols = self.part.shape
        split = self.grad.astype(BF16).reshape(group, 2, rows, cols)
        for h in range(2):
            self.part[h] = split[:, h]
        self.one().start()

    def second(self):
        self.one().wait_recv()
        total = self.part[lax.rem(self.d, 2)].astype(F32) + self.in1[...].astype(F32)
        cols = self.half.shape[-1]
        for h in range(2):
            self.half[h] = total[..., h * cols:(h + 1) * cols].astype(BF16)
        self.two().start()

    def third(self):
        self.two().wait_recv()
        total = self.half[self.d // 2].astype(F32) + self.in2[...].astype(F32)
        self.quarter[...] = total.astype(BF16)
        for g in self.members:
            self.three(g, self.me).start()
        self.in3[self.me] = self.quarter[self.me]

    def fourth(self):
        for g in self.members:
            self.three(g, g).wait_recv()
        self.done[self.d] = jnp.sum(self.in3[...].astype(F32), 0).astype(BF16)
        for c in self.others:
            self.four(c, self.d).start()

    def finish(self):
        for c in self.others:
            self.four(c, c).wait_recv()
        count, rows, cols = self.done.shape
        for c in range(count):
            self.out[pl.ds((c % 2) * rows, rows), pl.ds((c // 2) * cols, cols)] = self.done[c].astype(F32)
        self.one().wait_send()
        self.two().wait_send()
        for g in self.members:
            self.three(g, self.me).wait_send()
        for c in self.others:
            self.four(c, self.d).wait_send()


def sum_scratch(shape, group, clips):
    dma = pltpu.SemaphoreType.DMA
    rows, cols = shape[0] // group // 2, shape[1]
    return [
        pltpu.VMEM((2, group, rows, cols), BF16),
        pltpu.VMEM((group, rows, cols), BF16),
        pltpu.VMEM((2, group, rows, cols // 2), BF16),
        pltpu.VMEM((group, rows, cols // 2), BF16),
        pltpu.VMEM((group, rows, cols // 2), BF16),
        pltpu.VMEM((group, rows, cols // 2), BF16),
        pltpu.VMEM((clips, rows, cols // 2), BF16),
        dma((4,)),
        dma((group,)),
        dma((group,)),
        dma((clips,)),
        dma((clips,)),
    ]


def kernel(
    frames, spaces, clips, reduce, scale_mid, scale_top,
    feats, w_sp, w_tm, teach, w_dn, w_q, w_k, w_v, w_o, teach_top,
    student_out, gt_out, go_out,
    home, v_sp, v_tm, v_dn, v_q, v_k, v_v, v_o,
    cells, edge_send, edges, edge_near, shifted, spat, turned, teacher, teacher_top, mid32, stu,
    in_sem, own_sem, fs, fr, es, er, ts, tr, ps, pr_, ss, sr, hs, hr,
    *sums,
):
    t = lax.axis_index("tm")
    s = lax.axis_index("space")
    rows, _, wc, chan = feats.shape
    half_rows, _, hc, width = teach_top.shape
    peers = [lax.rem(t + i, frames) for i in range(1, frames)]
    group = frames * spaces
    me = t * spaces + s
    members = [lax.rem(me + i, group) for i in range(1, group)]
    d = lax.axis_index("dp")
    others = [lax.rem(d + i, clips) for i in range(1, clips)]

    loads = [
        pltpu.make_async_copy(src, dst, in_sem.at[i])
        for i, (src, dst) in enumerate(
            ((feats, home), (w_sp, v_sp), (w_tm, v_tm), (w_dn, v_dn),
             (w_q, v_q), (w_k, v_k), (w_v, v_v), (w_o, v_o))
        )
    ]
    for load in loads:
        load.start()
    own = [
        pltpu.make_async_copy(feats.at[:, t], cells.at[pl.ds(1, rows), t], own_sem.at[0]),
        pltpu.make_async_copy(teach.at[:, t], teacher.at[t], own_sem.at[1]),
        pltpu.make_async_copy(teach_top.at[:, t], teacher_top.at[t], own_sem.at[2]),
    ]
    for copy in own:
        copy.start()

    barrier = pltpu.get_barrier_semaphore()
    for g in members:
        pl.semaphore_signal(
            barrier, inc=1, device_id={"tm": g // spaces, "space": lax.rem(g, spaces)},
            device_id_type=MESH,
        )
    if reduce:
        for c in others:
            pl.semaphore_signal(barrier, inc=1, device_id={"dp": c}, device_id_type=MESH)

    loads[0].wait()
    for u in range(frames):
        if u > 0:
            left = home[:, u - 1, wc - 8:, :].astype(F32)[:, 7, :]
        else:
            left = jnp.zeros((rows, chan), F32)
        if u < frames - 1:
            right = home[:, u + 1, :8, :].astype(F32)[:, 0, :]
        else:
            right = jnp.zeros((rows, chan), F32)
        edge_send[u] = jnp.concatenate([left, right], 0).astype(BF16)

    pl.semaphore_wait(barrier, group - 1 + (clips - 1 if reduce else 0))

    def send(src, dst, ssem, rsem, u):
        return pltpu.make_async_remote_copy(
            src_ref=src, dst_ref=dst, send_sem=ssem, recv_sem=rsem,
            device_id={"tm": u}, device_id_type=MESH,
        )

    def feats_copy(u, f):
        return send(home.at[:, u], cells.at[pl.ds(1, rows), f], fs.at[u], fr.at[f], u)

    def edge_copy(u, f):
        return send(edge_send.at[u], edges.at[f], es.at[u], er.at[f], u)

    def teach_copy(u, f, h):
        part = pl.ds(h * (rows // 2), rows // 2)
        return send(teach.at[part, u], teacher.at[f, part],
                    ts.at[h * frames + u], tr.at[h * frames + f], u)

    def top_copy(u, f):
        return send(teach_top.at[:, u], teacher_top.at[f], ps.at[u], pr_.at[f], u)

    def student_copy(u, f):
        return send(stu.at[u], student_out.at[:, f], ss.at[u], sr.at[f], u)

    for u in peers:
        edge_copy(u, t).start()
        feats_copy(u, t).start()
    edges[t] = edge_send[t]
    spat[pl.ds(0, 2)] = jnp.zeros((2,) + spat.shape[1:], BF16)

    @pl.when(s == 0)
    def _():
        cells[0] = jnp.zeros(cells.shape[1:], BF16)
        edge_near[0] = jnp.zeros(edges.shape, BF16)

    @pl.when(s == spaces - 1)
    def _():
        cells[rows + 1] = jnp.zeros(cells.shape[1:], BF16)
        edge_near[1] = jnp.zeros(edges.shape, BF16)

    own[0].wait()
    for f in peers:
        edge_copy(f, f).wait_recv()
        feats_copy(f, f).wait_recv()
    for u in peers:
        top_copy(u, t).start()
    for h in range(2):
        for u in peers:
            teach_copy(u, t, h).start()

    def halo(src, dst, i, j, to):
        return pltpu.make_async_remote_copy(
            src_ref=src, dst_ref=dst, send_sem=hs.at[i], recv_sem=hr.at[j],
            device_id={"space": to}, device_id_type=MESH,
        )

    def up(to):
        return (halo(cells.at[1], cells.at[rows + 1], 0, 0, to),
                halo(edges, edge_near.at[1], 1, 1, to))

    def down(to):
        return (halo(cells.at[rows], cells.at[0], 2, 2, to),
                halo(edges, edge_near.at[0], 3, 3, to))

    @pl.when(s > 0)
    def _():
        for copy in up(s - 1):
            copy.start()

    @pl.when(s < spaces - 1)
    def _():
        for copy in down(s + 1):
            copy.start()

    column = lax.broadcasted_iota(jnp.int32, (frames, wc, chan), 1)

    def shift(row, left, right):
        x = cells[row].astype(F32)
        a = jnp.where(column == 0, left, pltpu.roll(x, 1, 1))
        b = jnp.where(column == wc - 1, right, pltpu.roll(x, wc - 1, 1))
        flat = (frames * wc, chan)
        shifted[row, :, pl.ds(0, chan)] = a.astype(BF16).reshape(flat)
        shifted[row, :, pl.ds(chan, chan)] = cells[row].reshape(flat)
        shifted[row, :, pl.ds(2 * chan, chan)] = b.astype(BF16).reshape(flat)

    def conv(first, count):
        total = None
        for dy in range(3):
            block = shifted[pl.ds(first + dy, count)].reshape(count * frames * wc, 3 * chan)
            term = dot(block, v_sp[dy])
            total = term if total is None else total + term
        out = (total / (1.0 + jnp.exp(-total))).astype(BF16)
        out = out.reshape(count, frames, wc, chan)
        for i in range(count):
            spat[pl.ds(2, frames), first + i] = out[i]

    side = edges[...].astype(F32)
    for r in range(rows):
        shift(r + 1, side[:, r:r + 1, :], side[:, rows + r:rows + r + 1, :])
    loads[1].wait()
    conv(1, rows - 2)

    @pl.when(s < spaces - 1)
    def _():
        for copy in up(s + 1):
            copy.wait_recv()

    @pl.when(s > 0)
    def _():
        for copy in down(s - 1):
            copy.wait_recv()

    side = edge_near[0].astype(F32)
    shift(0, side[:, rows - 1:rows, :], side[:, 2 * rows - 1:2 * rows, :])
    side = edge_near[1].astype(F32)
    shift(rows + 1, side[:, 0:1, :], side[:, rows:rows + 1, :])
    conv(0, 1)
    conv(rows - 1, 1)

    loads[2].wait()
    half = chan // 2
    n = frames * rows * wc
    total = None
    for k in range(3):
        term = dot(spat[pl.ds(k, frames)].reshape(n, chan), v_tm[pl.ds(k * chan, chan), :])
        total = term if total is None else total + term
    for f in range(frames):
        base = cells[pl.ds(1, rows), f].astype(F32).reshape(rows * wc, chan)
        span = slice(f * rows * wc, (f + 1) * rows * wc)
        mid = (base + total[span]).astype(BF16).astype(F32)
        for h in range(2):
            mid32[h, span, :] = mid[:, h * half:(h + 1) * half]

    loads[3].wait()
    coarse = None
    count = frames * rows * wc // 2
    for b in range(2):
        part = jnp.concatenate(
            [mid32[h, pl.ds(b, count, stride=2), :] for h in range(2)], -1
        ).reshape(frames * half_rows, 2, hc, chan)
        for a in range(2):
            block = part[:, a].reshape(frames * half_rows * hc, chan).astype(BF16)
            term = dot(block, v_dn[a, b])
            coarse = term if coarse is None else coarse + term
    coarse = coarse.astype(BF16)

    for i in range(4, 8):
        loads[i].wait()
    points = half_rows * hc
    query = dot(coarse, v_q[...]).astype(BF16).astype(F32).reshape(frames, points, width)
    key = dot(coarse, v_k[...]).astype(BF16).astype(F32).reshape(frames, points, width)
    value = dot(coarse, v_v[...]).astype(BF16).astype(F32).reshape(frames, points, width)
    scale = 1.0 / math.sqrt(width)
    results = []
    for q in range(frames):
        score = [jnp.sum(query[q] * key[k], -1, keepdims=True) * scale for k in range(q + 1)]
        top = functools.reduce(jnp.maximum, score)
        weight = [jnp.exp(x - top) for x in score]
        total = functools.reduce(jnp.add, weight)
        acc = functools.reduce(jnp.add, [weight[k] * value[k] for k in range(q + 1)])
        results.append(acc / total)
    attended = jnp.concatenate(results, 0).astype(BF16)
    student = (coarse.astype(F32) + dot(attended, v_o[...])).astype(BF16)
    stu[...] = student.reshape(frames, half_rows, hc, width)
    keep = pltpu.make_async_copy(stu.at[t], student_out.at[:, t], own_sem.at[3])
    keep.start()

    for u in peers:
        student_copy(u, t).start()

    turned_top = attended.T
    own[2].wait()
    for f in peers:
        top_copy(f, f).wait_recv()
    diff_top = (
        student.astype(F32) - teacher_top[...].astype(F32).reshape(frames * points, width)
    ).astype(BF16)
    grad_top = dot(turned_top, diff_top) * scale_top
    if reduce:
        top_sum = Sum(sums[12:], go_out, grad_top, d, me, members, others, spaces)
        top_sum.first()
    else:
        go_out[...] = grad_top

    low = rows // 2
    for h in range(2):
        for k in range(3):
            part = spat[pl.ds(k, frames), pl.ds(h * low, low)]
            turned[h, k] = part.reshape(n // 2, chan).T
    if reduce:
        top_sum.second()
    own[1].wait()
    grad = [None] * 3
    for h in range(2):
        for f in peers:
            teach_copy(f, f, h).wait_recv()
        mid = jnp.concatenate(
            [mid32[i].reshape(frames, 2, low * wc, half)[:, h] for i in range(2)], -1
        ).reshape(n // 2, chan)
        diff = mid - teacher[:, pl.ds(h * low, low)].astype(F32).reshape(n // 2, chan)
        for k in range(3):
            term = dot(turned[h, k], diff.astype(BF16))
            grad[k] = term if h == 0 else grad[k] + term
        if reduce and h == 0:
            top_sum.third()
    grad = jnp.concatenate(grad, 0) * scale_mid
    if reduce:
        mid_sum = Sum(sums[:12], gt_out, grad, d, me, members, others, spaces)
        mid_sum.first()
        top_sum.fourth()
        mid_sum.second()
        mid_sum.third()
        top_sum.finish()
        mid_sum.fourth()
        mid_sum.finish()
    else:
        gt_out[...] = grad

    keep.wait()
    for u in peers:
        student_copy(u, u).wait_recv()
    for u in peers:
        edge_copy(u, t).wait_send()
        feats_copy(u, t).wait_send()
        for h in range(2):
            teach_copy(u, t, h).wait_send()
        top_copy(u, t).wait_send()
        student_copy(u, t).wait_send()

    @pl.when(s > 0)
    def _():
        for copy in up(s - 1):
            copy.wait_send()

    @pl.when(s < spaces - 1)
    def _():
        for copy in down(s + 1):
            copy.wait_send()


def hand_over(*refs):
    count = (len(refs) - 1) // 3
    ins, outs, held, sems = refs[:count], refs[count:2 * count], refs[2 * count:-1], refs[-1]
    reads = [pltpu.make_async_copy(ins[i], held[i], sems.at[0, i]) for i in range(count)]
    writes = [pltpu.make_async_copy(held[i], outs[i], sems.at[1, i]) for i in range(count)]
    for copy in reads:
        copy.start()
    for i in range(count):
        reads[i].wait()
        writes[i].start()
    for copy in writes:
        copy.wait()


def local(
    feats, w_spatial, w_temporal, teacher_mid, w_down, w_query, w_key, w_value, w_out, teacher_top
):
    frames = lax.axis_size("tm")
    spaces = lax.axis_size("space")
    devices_all = lax.axis_size("dp") * frames * spaces
    rows, cols, chan = feats.shape[2:]
    half_rows, half_cols, width = teacher_top.shape[2:]
    wc, hc = cols // frames, half_cols // frames
    scale_mid = 1.0 / math.sqrt(rows * cols * devices_all)
    scale_top = 1.0 / math.sqrt(half_rows * half_cols * devices_all)
    dma = pltpu.SemaphoreType.DMA
    group, clips = frames * spaces, lax.axis_size("dp")
    grads = (w_temporal.shape, w_out.shape)
    reduce = clips == 4 and all(r % (32 * group) == 0 and c % 256 == 0 for r, c in grads)
    pieces = [(r // group, c) if reduce else (r, c) for r, c in grads]
    student, gt, go = pl.pallas_call(
        functools.partial(kernel, frames, spaces, clips, reduce, scale_mid, scale_top),
        out_shape=(
            jax.ShapeDtypeStruct((half_rows, frames, hc, width), BF16),
            jax.ShapeDtypeStruct(pieces[0], F32),
            jax.ShapeDtypeStruct(pieces[1], F32),
        ),
        in_specs=[pl.BlockSpec(memory_space=pl.ANY)] * 10,
        out_specs=(
            pl.BlockSpec(memory_space=pl.ANY),
            pl.BlockSpec(memory_space=pltpu.VMEM),
            pl.BlockSpec(memory_space=pltpu.VMEM),
        ),
        scratch_shapes=[
            pltpu.VMEM((rows, frames, wc, chan), BF16),
            pltpu.VMEM((3, 3 * chan, chan), BF16),
            pltpu.VMEM(w_temporal.shape, BF16),
            pltpu.VMEM(w_down.shape, BF16),
            pltpu.VMEM(w_query.shape, BF16),
            pltpu.VMEM(w_key.shape, BF16),
            pltpu.VMEM(w_value.shape, BF16),
            pltpu.VMEM(w_out.shape, BF16),
            pltpu.VMEM((rows + 2, frames, wc, chan), BF16),
            pltpu.VMEM((frames, 2 * rows, chan), BF16),
            pltpu.VMEM((frames, 2 * rows, chan), BF16),
            pltpu.VMEM((2, frames, 2 * rows, chan), BF16),
            pltpu.VMEM((rows + 2, frames * wc, 3 * chan), BF16),
            pltpu.VMEM((frames + 2, rows, wc, chan), BF16),
            pltpu.VMEM((2, 3, chan, frames * rows * wc // 2), BF16),
            pltpu.VMEM((frames, rows, wc, chan), BF16),
            pltpu.VMEM((frames, half_rows, hc, width), BF16),
            pltpu.VMEM((2, frames * rows * wc, chan // 2), F32),
            pltpu.VMEM((frames, half_rows, hc, width), BF16),
            dma((8,)),
            dma((4,)),
        ]
        + [dma((frames,))] * 4
        + [dma((2 * frames,))] * 2
        + [dma((frames,))] * 4
        + [dma((4,)), dma((4,))]
        + (sum_scratch(grads[0], group, clips) + sum_scratch(grads[1], group, clips) if reduce else []),
        compiler_params=pltpu.CompilerParams(
            collective_id=0, has_side_effects=True, vmem_limit_bytes=58 * 1024 * 1024
        ),
    )(
        feats.reshape(rows, frames, wc, chan),
        w_spatial.reshape(3, 3 * chan, chan),
        w_temporal,
        teacher_mid.reshape(rows, frames, wc, chan),
        w_down,
        w_query,
        w_key,
        w_value,
        w_out,
        teacher_top.reshape(half_rows, frames, hc, width),
    )
    if reduce:
        student, gt, go = pl.pallas_call(
            hand_over,
            out_shape=tuple(jax.ShapeDtypeStruct(x.shape, x.dtype) for x in (student, gt, go)),
            in_specs=[pl.BlockSpec(memory_space=pl.ANY)] * 3,
            out_specs=(pl.BlockSpec(memory_space=pl.ANY),) * 3,
            scratch_shapes=[pltpu.VMEM(x.shape, x.dtype) for x in (student, gt, go)]
            + [dma((2, 3))],
            compiler_params=pltpu.CompilerParams(vmem_limit_bytes=58 * 1024 * 1024),
        )(student, gt, go)
    else:
        gt = lax.psum_scatter(gt, ("tm", "space"), scatter_dimension=0, tiled=True)
        go = lax.psum_scatter(go, ("tm", "space"), scatter_dimension=0, tiled=True)
        gt, go = lax.psum((gt, go), "dp")
    return (student.reshape(1, 1, half_rows, half_cols, width), gt, go)


def solution(mesh):
    frame = P("dp", "tm", "space", None, None)
    return jax.shard_map(
        local,
        mesh=mesh,
        in_specs=(frame, P(), P(), frame, P(), P(), P(), P(), P(), frame),
        out_specs=(frame, P(("tm", "space"), None), P(("tm", "space"), None)),
        check_vma=False,
    )
```

```python
import functools
import math

import jax
import jax.numpy as jnp
from jax import lax
from jax.experimental import pallas as pl
from jax.experimental.pallas import tpu as pltpu
from jax.sharding import PartitionSpec as P

MESH = pl.DeviceIdType.MESH
F32 = jnp.float32
BF16 = jnp.bfloat16


def dot(a, b):
    return jnp.dot(a, b, preferred_element_type=F32)


class Sum:
    def __init__(self, refs, out, grad, d, me, members, others, spaces):
        (self.part, self.in1, self.half, self.in2, self.quarter, self.in3, self.done,
         self.sem12, self.s3, self.r3, self.s4, self.r4) = refs
        self.out, self.grad, self.d, self.me = out, grad, d, me
        self.members, self.others, self.spaces = members, others, spaces

    def copy(self, src, dst, ssem, rsem, to):
        return pltpu.make_async_remote_copy(
            src_ref=src, dst_ref=dst, send_sem=ssem, recv_sem=rsem,
            device_id=to, device_id_type=MESH,
        )

    def one(self):
        low = lax.rem(self.d, 2)
        return self.copy(self.part.at[1 - low], self.in1, self.sem12.at[0], self.sem12.at[1],
                         {"dp": self.d + 1 - 2 * low})

    def two(self):
        high = self.d // 2
        return self.copy(self.half.at[1 - high], self.in2, self.sem12.at[2], self.sem12.at[3],
                         {"dp": self.d + 2 - 4 * high})

    def three(self, g, f):
        return self.copy(self.quarter.at[g], self.in3.at[f], self.s3.at[g], self.r3.at[f],
                         {"tm": g // self.spaces, "space": lax.rem(g, self.spaces)})

    def four(self, c, f):
        return self.copy(self.done.at[f], self.done.at[f], self.s4.at[c], self.r4.at[f],
                         {"dp": c})

    def first(self):
        _, group, rows, cols = self.part.shape
        split = self.grad.astype(BF16).reshape(group, 2, rows, cols)
        for h in range(2):
            self.part[h] = split[:, h]
        self.one().start()

    def second(self):
        self.one().wait_recv()
        total = self.part[lax.rem(self.d, 2)].astype(F32) + self.in1[...].astype(F32)
        cols = self.half.shape[-1]
        for h in range(2):
            self.half[h] = total[..., h * cols:(h + 1) * cols].astype(BF16)
        self.two().start()

    def third(self):
        self.two().wait_recv()
        total = self.half[self.d // 2].astype(F32) + self.in2[...].astype(F32)
        self.quarter[...] = total.astype(BF16)
        for g in self.members:
            self.three(g, self.me).start()
        self.in3[self.me] = self.quarter[self.me]

    def fourth(self):
        for g in self.members:
            self.three(g, g).wait_recv()
        self.done[self.d] = jnp.sum(self.in3[...].astype(F32), 0).astype(BF16)
        for c in self.others:
            self.four(c, self.d).start()

    def finish(self):
        for c in self.others:
            self.four(c, c).wait_recv()
        count, rows, cols = self.done.shape
        for c in range(count):
            self.out[pl.ds((c % 2) * rows, rows), pl.ds((c // 2) * cols, cols)] = self.done[c].astype(F32)
        self.one().wait_send()
        self.two().wait_send()
        for g in self.members:
            self.three(g, self.me).wait_send()
        for c in self.others:
            self.four(c, self.d).wait_send()


def sum_scratch(shape, group, clips):
    dma = pltpu.SemaphoreType.DMA
    rows, cols = shape[0] // group // 2, shape[1]
    return [
        pltpu.VMEM((2, group, rows, cols), BF16),
        pltpu.VMEM((group, rows, cols), BF16),
        pltpu.VMEM((2, group, rows, cols // 2), BF16),
        pltpu.VMEM((group, rows, cols // 2), BF16),
        pltpu.VMEM((group, rows, cols // 2), BF16),
        pltpu.VMEM((group, rows, cols // 2), BF16),
        pltpu.VMEM((clips, rows, cols // 2), BF16),
        dma((4,)),
        dma((group,)),
        dma((group,)),
        dma((clips,)),
        dma((clips,)),
    ]


def kernel(
    frames, spaces, clips, reduce, scale_mid, scale_top,
    feats, w_sp, w_tm, teach, w_dn, w_q, w_k, w_v, w_o, teach_top,
    student_out, gt_out, go_out,
    home, v_sp, v_tm, v_dn, v_q, v_k, v_v, v_o,
    cells, edge_send, edges, edge_near, shifted, spat, turned, teacher, teacher_top, mid32, stu,
    in_sem, own_sem, fs, fr, es, er, ts, tr, ps, pr_, ss, sr, hs, hr,
    *sums,
):
    t = lax.axis_index("tm")
    s = lax.axis_index("space")
    rows, _, wc, chan = feats.shape
    half_rows, _, hc, width = teach_top.shape
    peers = [lax.rem(t + i, frames) for i in range(1, frames)]
    group = frames * spaces
    me = t * spaces + s
    members = [lax.rem(me + i, group) for i in range(1, group)]
    d = lax.axis_index("dp")
    others = [lax.rem(d + i, clips) for i in range(1, clips)]

    loads = [
        pltpu.make_async_copy(src, dst, in_sem.at[i])
        for i, (src, dst) in enumerate(
            ((feats, home), (w_sp, v_sp), (w_tm, v_tm), (w_dn, v_dn),
             (w_q, v_q), (w_k, v_k), (w_v, v_v), (w_o, v_o))
        )
    ]
    for load in loads:
        load.start()
    own = [
        pltpu.make_async_copy(feats.at[:, t], cells.at[pl.ds(1, rows), t], own_sem.at[0]),
        pltpu.make_async_copy(teach.at[:, t], teacher.at[t], own_sem.at[1]),
        pltpu.make_async_copy(teach_top.at[:, t], teacher_top.at[t], own_sem.at[2]),
    ]
    for copy in own:
        copy.start()

    barrier = pltpu.get_barrier_semaphore()
    for g in members:
        pl.semaphore_signal(
            barrier, inc=1, device_id={"tm": g // spaces, "space": lax.rem(g, spaces)},
            device_id_type=MESH,
        )
    if reduce:
        for c in others:
            pl.semaphore_signal(barrier, inc=1, device_id={"dp": c}, device_id_type=MESH)

    loads[0].wait()
    for u in range(frames):
        if u > 0:
            left = home[:, u - 1, wc - 8:, :].astype(F32)[:, 7, :]
        else:
            left = jnp.zeros((rows, chan), F32)
        if u < frames - 1:
            right = home[:, u + 1, :8, :].astype(F32)[:, 0, :]
        else:
            right = jnp.zeros((rows, chan), F32)
        edge_send[u] = jnp.concatenate([left, right], 0).astype(BF16)

    pl.semaphore_wait(barrier, group - 1 + (clips - 1 if reduce else 0))

    def send(src, dst, ssem, rsem, u):
        return pltpu.make_async_remote_copy(
            src_ref=src, dst_ref=dst, send_sem=ssem, recv_sem=rsem,
            device_id={"tm": u}, device_id_type=MESH,
        )

    def feats_copy(u, f):
        return send(home.at[:, u], cells.at[pl.ds(1, rows), f], fs.at[u], fr.at[f], u)

    def edge_copy(u, f):
        return send(edge_send.at[u], edges.at[f], es.at[u], er.at[f], u)

    def teach_copy(u, f, h):
        part = pl.ds(h * (rows // 2), rows // 2)
        return send(teach.at[part, u], teacher.at[f, part],
                    ts.at[h * frames + u], tr.at[h * frames + f], u)

    def top_copy(u, f):
        return send(teach_top.at[:, u], teacher_top.at[f], ps.at[u], pr_.at[f], u)

    def student_copy(u, f):
        return send(stu.at[u], student_out.at[:, f], ss.at[u], sr.at[f], u)

    for u in peers:
        edge_copy(u, t).start()
        feats_copy(u, t).start()
    edges[t] = edge_send[t]
    spat[pl.ds(0, 2)] = jnp.zeros((2,) + spat.shape[1:], BF16)

    @pl.when(s == 0)
    def _():
        cells[0] = jnp.zeros(cells.shape[1:], BF16)
        edge_near[0] = jnp.zeros(edges.shape, BF16)

    @pl.when(s == spaces - 1)
    def _():
        cells[rows + 1] = jnp.zeros(cells.shape[1:], BF16)
        edge_near[1] = jnp.zeros(edges.shape, BF16)

    own[0].wait()
    for f in peers:
        edge_copy(f, f).wait_recv()
        feats_copy(f, f).wait_recv()
    for u in peers:
        top_copy(u, t).start()
    for h in range(2):
        for u in peers:
            teach_copy(u, t, h).start()

    def halo(src, dst, i, j, to):
        return pltpu.make_async_remote_copy(
            src_ref=src, dst_ref=dst, send_sem=hs.at[i], recv_sem=hr.at[j],
            device_id={"space": to}, device_id_type=MESH,
        )

    def up(to):
        return (halo(cells.at[1], cells.at[rows + 1], 0, 0, to),
                halo(edges, edge_near.at[1], 1, 1, to))

    def down(to):
        return (halo(cells.at[rows], cells.at[0], 2, 2, to),
                halo(edges, edge_near.at[0], 3, 3, to))

    @pl.when(s > 0)
    def _():
        for copy in up(s - 1):
            copy.start()

    @pl.when(s < spaces - 1)
    def _():
        for copy in down(s + 1):
            copy.start()

    column = lax.broadcasted_iota(jnp.int32, (frames, wc, chan), 1)

    def shift(row, left, right):
        x = cells[row].astype(F32)
        a = jnp.where(column == 0, left, pltpu.roll(x, 1, 1))
        b = jnp.where(column == wc - 1, right, pltpu.roll(x, wc - 1, 1))
        flat = (frames * wc, chan)
        shifted[row, :, pl.ds(0, chan)] = a.astype(BF16).reshape(flat)
        shifted[row, :, pl.ds(chan, chan)] = cells[row].reshape(flat)
        shifted[row, :, pl.ds(2 * chan, chan)] = b.astype(BF16).reshape(flat)

    def conv(first, count):
        total = None
        for dy in range(3):
            block = shifted[pl.ds(first + dy, count)].reshape(count * frames * wc, 3 * chan)
            term = dot(block, v_sp[dy])
            total = term if total is None else total + term
        out = (total / (1.0 + jnp.exp(-total))).astype(BF16)
        out = out.reshape(count, frames, wc, chan)
        for i in range(count):
            spat[pl.ds(2, frames), first + i] = out[i]

    side = edges[...].astype(F32)
    for r in range(rows):
        shift(r + 1, side[:, r:r + 1, :], side[:, rows + r:rows + r + 1, :])
    loads[1].wait()
    conv(1, rows - 2)

    @pl.when(s < spaces - 1)
    def _():
        for copy in up(s + 1):
            copy.wait_recv()

    @pl.when(s > 0)
    def _():
        for copy in down(s - 1):
            copy.wait_recv()

    side = edge_near[0].astype(F32)
    shift(0, side[:, rows - 1:rows, :], side[:, 2 * rows - 1:2 * rows, :])
    side = edge_near[1].astype(F32)
    shift(rows + 1, side[:, 0:1, :], side[:, rows:rows + 1, :])
    conv(0, 1)
    conv(rows - 1, 1)

    loads[2].wait()
    half = chan // 2
    n = frames * rows * wc
    total = None
    for k in range(3):
        term = dot(spat[pl.ds(k, frames)].reshape(n, chan), v_tm[pl.ds(k * chan, chan), :])
        total = term if total is None else total + term
    for f in range(frames):
        base = cells[pl.ds(1, rows), f].astype(F32).reshape(rows * wc, chan)
        span = slice(f * rows * wc, (f + 1) * rows * wc)
        mid = (base + total[span]).astype(BF16).astype(F32)
        for h in range(2):
            mid32[h, span, :] = mid[:, h * half:(h + 1) * half]

    loads[3].wait()
    coarse = None
    count = frames * rows * wc // 2
    for b in range(2):
        part = jnp.concatenate(
            [mid32[h, pl.ds(b, count, stride=2), :] for h in range(2)], -1
        ).reshape(frames * half_rows, 2, hc, chan)
        for a in range(2):
            block = part[:, a].reshape(frames * half_rows * hc, chan).astype(BF16)
            term = dot(block, v_dn[a, b])
            coarse = term if coarse is None else coarse + term
    coarse = coarse.astype(BF16)

    for i in range(4, 8):
        loads[i].wait()
    points = half_rows * hc
    query = dot(coarse, v_q[...]).astype(BF16).astype(F32).reshape(frames, points, width)
    key = dot(coarse, v_k[...]).astype(BF16).astype(F32).reshape(frames, points, width)
    value = dot(coarse, v_v[...]).astype(BF16).astype(F32).reshape(frames, points, width)
    scale = 1.0 / math.sqrt(width)
    results = []
    for q in range(frames):
        score = [jnp.sum(query[q] * key[k], -1, keepdims=True) * scale for k in range(q + 1)]
        top = functools.reduce(jnp.maximum, score)
        weight = [jnp.exp(x - top) for x in score]
        total = functools.reduce(jnp.add, weight)
        acc = functools.reduce(jnp.add, [weight[k] * value[k] for k in range(q + 1)])
        results.append(acc / total)
    attended = jnp.concatenate(results, 0).astype(BF16)
    student = (coarse.astype(F32) + dot(attended, v_o[...])).astype(BF16)
    stu[...] = student.reshape(frames, half_rows, hc, width)
    keep = pltpu.make_async_copy(stu.at[t], student_out.at[:, t], own_sem.at[3])
    keep.start()


    turned_top = attended.T
    own[2].wait()
    for f in peers:
        top_copy(f, f).wait_recv()
    diff_top = (
        student.astype(F32) - teacher_top[...].astype(F32).reshape(frames * points, width)
    ).astype(BF16)
    grad_top = dot(turned_top, diff_top) * scale_top
    if reduce:
        top_sum = Sum(sums[12:], go_out, grad_top, d, me, members, others, spaces)
        top_sum.first()
    else:
        go_out[...] = grad_top

    low = rows // 2
    for h in range(2):
        for k in range(3):
            part = spat[pl.ds(k, frames), pl.ds(h * low, low)]
            turned[h, k] = part.reshape(n // 2, chan).T
    if reduce:
        top_sum.second()
    own[1].wait()
    grad = [None] * 3
    for h in range(2):
        for f in peers:
            teach_copy(f, f, h).wait_recv()
        if h == 1:
            for u in peers:
                student_copy(u, t).start()
        mid = jnp.concatenate(
            [mid32[i].reshape(frames, 2, low * wc, half)[:, h] for i in range(2)], -1
        ).reshape(n // 2, chan)
        diff = mid - teacher[:, pl.ds(h * low, low)].astype(F32).reshape(n // 2, chan)
        for k in range(3):
            term = dot(turned[h, k], diff.astype(BF16))
            grad[k] = term if h == 0 else grad[k] + term
        if reduce and h == 0:
            top_sum.third()
    grad = jnp.concatenate(grad, 0) * scale_mid
    if reduce:
        mid_sum = Sum(sums[:12], gt_out, grad, d, me, members, others, spaces)
        mid_sum.first()
        top_sum.fourth()
        mid_sum.second()
        mid_sum.third()
        top_sum.finish()
        mid_sum.fourth()
        mid_sum.finish()
    else:
        gt_out[...] = grad

    keep.wait()
    for u in peers:
        student_copy(u, u).wait_recv()
    for u in peers:
        edge_copy(u, t).wait_send()
        feats_copy(u, t).wait_send()
        for h in range(2):
            teach_copy(u, t, h).wait_send()
        top_copy(u, t).wait_send()
        student_copy(u, t).wait_send()

    @pl.when(s > 0)
    def _():
        for copy in up(s - 1):
            copy.wait_send()

    @pl.when(s < spaces - 1)
    def _():
        for copy in down(s + 1):
            copy.wait_send()


def hand_over(*refs):
    count = (len(refs) - 1) // 3
    ins, outs, held, sems = refs[:count], refs[count:2 * count], refs[2 * count:-1], refs[-1]
    reads = [pltpu.make_async_copy(ins[i], held[i], sems.at[0, i]) for i in range(count)]
    writes = [pltpu.make_async_copy(held[i], outs[i], sems.at[1, i]) for i in range(count)]
    for copy in reads:
        copy.start()
    for i in range(count):
        reads[i].wait()
        writes[i].start()
    for copy in writes:
        copy.wait()


def local(
    feats, w_spatial, w_temporal, teacher_mid, w_down, w_query, w_key, w_value, w_out, teacher_top
):
    frames = lax.axis_size("tm")
    spaces = lax.axis_size("space")
    devices_all = lax.axis_size("dp") * frames * spaces
    rows, cols, chan = feats.shape[2:]
    half_rows, half_cols, width = teacher_top.shape[2:]
    wc, hc = cols // frames, half_cols // frames
    scale_mid = 1.0 / math.sqrt(rows * cols * devices_all)
    scale_top = 1.0 / math.sqrt(half_rows * half_cols * devices_all)
    dma = pltpu.SemaphoreType.DMA
    group, clips = frames * spaces, lax.axis_size("dp")
    grads = (w_temporal.shape, w_out.shape)
    reduce = clips == 4 and all(r % (32 * group) == 0 and c % 256 == 0 for r, c in grads)
    pieces = [(r // group, c) if reduce else (r, c) for r, c in grads]
    student, gt, go = pl.pallas_call(
        functools.partial(kernel, frames, spaces, clips, reduce, scale_mid, scale_top),
        out_shape=(
            jax.ShapeDtypeStruct((half_rows, frames, hc, width), BF16),
            jax.ShapeDtypeStruct(pieces[0], F32),
            jax.ShapeDtypeStruct(pieces[1], F32),
        ),
        in_specs=[pl.BlockSpec(memory_space=pl.ANY)] * 10,
        out_specs=(
            pl.BlockSpec(memory_space=pl.ANY),
            pl.BlockSpec(memory_space=pltpu.VMEM),
            pl.BlockSpec(memory_space=pltpu.VMEM),
        ),
        scratch_shapes=[
            pltpu.VMEM((rows, frames, wc, chan), BF16),
            pltpu.VMEM((3, 3 * chan, chan), BF16),
            pltpu.VMEM(w_temporal.shape, BF16),
            pltpu.VMEM(w_down.shape, BF16),
            pltpu.VMEM(w_query.shape, BF16),
            pltpu.VMEM(w_key.shape, BF16),
            pltpu.VMEM(w_value.shape, BF16),
            pltpu.VMEM(w_out.shape, BF16),
            pltpu.VMEM((rows + 2, frames, wc, chan), BF16),
            pltpu.VMEM((frames, 2 * rows, chan), BF16),
            pltpu.VMEM((frames, 2 * rows, chan), BF16),
            pltpu.VMEM((2, frames, 2 * rows, chan), BF16),
            pltpu.VMEM((rows + 2, frames * wc, 3 * chan), BF16),
            pltpu.VMEM((frames + 2, rows, wc, chan), BF16),
            pltpu.VMEM((2, 3, chan, frames * rows * wc // 2), BF16),
            pltpu.VMEM((frames, rows, wc, chan), BF16),
            pltpu.VMEM((frames, half_rows, hc, width), BF16),
            pltpu.VMEM((2, frames * rows * wc, chan // 2), F32),
            pltpu.VMEM((frames, half_rows, hc, width), BF16),
            dma((8,)),
            dma((4,)),
        ]
        + [dma((frames,))] * 4
        + [dma((2 * frames,))] * 2
        + [dma((frames,))] * 4
        + [dma((4,)), dma((4,))]
        + (sum_scratch(grads[0], group, clips) + sum_scratch(grads[1], group, clips) if reduce else []),
        compiler_params=pltpu.CompilerParams(
            collective_id=0, has_side_effects=True, vmem_limit_bytes=58 * 1024 * 1024
        ),
    )(
        feats.reshape(rows, frames, wc, chan),
        w_spatial.reshape(3, 3 * chan, chan),
        w_temporal,
        teacher_mid.reshape(rows, frames, wc, chan),
        w_down,
        w_query,
        w_key,
        w_value,
        w_out,
        teacher_top.reshape(half_rows, frames, hc, width),
    )
    if reduce:
        student, gt, go = pl.pallas_call(
            hand_over,
            out_shape=tuple(jax.ShapeDtypeStruct(x.shape, x.dtype) for x in (student, gt, go)),
            in_specs=[pl.BlockSpec(memory_space=pl.ANY)] * 3,
            out_specs=(pl.BlockSpec(memory_space=pl.ANY),) * 3,
            scratch_shapes=[pltpu.VMEM(x.shape, x.dtype) for x in (student, gt, go)]
            + [dma((2, 3))],
            compiler_params=pltpu.CompilerParams(vmem_limit_bytes=58 * 1024 * 1024),
        )(student, gt, go)
    else:
        gt = lax.psum_scatter(gt, ("tm", "space"), scatter_dimension=0, tiled=True)
        go = lax.psum_scatter(go, ("tm", "space"), scatter_dimension=0, tiled=True)
        gt, go = lax.psum((gt, go), "dp")
    return (student.reshape(1, 1, half_rows, half_cols, width), gt, go)


def solution(mesh):
    frame = P("dp", "tm", "space", None, None)
    return jax.shard_map(
        local,
        mesh=mesh,
        in_specs=(frame, P(), P(), frame, P(), P(), P(), P(), P(), frame),
        out_specs=(frame, P(("tm", "space"), None), P(("tm", "space"), None)),
        check_vma=False,
    )
```

```python
import functools
import math

import jax
import jax.numpy as jnp
from jax import lax
from jax.experimental import pallas as pl
from jax.experimental.pallas import tpu as pltpu
from jax.sharding import PartitionSpec as P

MESH = pl.DeviceIdType.MESH
F32 = jnp.float32
BF16 = jnp.bfloat16


def dot(a, b):
    return jnp.dot(a, b, preferred_element_type=F32)


class Sum:
    def __init__(self, refs, out, grad, d, me, members, others, spaces):
        (self.part, self.in1, self.half, self.in2, self.quarter, self.in3, self.done,
         self.sem12, self.s3, self.r3, self.s4, self.r4) = refs
        self.out, self.grad, self.d, self.me = out, grad, d, me
        self.members, self.others, self.spaces = members, others, spaces

    def copy(self, src, dst, ssem, rsem, to):
        return pltpu.make_async_remote_copy(
            src_ref=src, dst_ref=dst, send_sem=ssem, recv_sem=rsem,
            device_id=to, device_id_type=MESH,
        )

    def one(self):
        low = lax.rem(self.d, 2)
        return self.copy(self.part.at[1 - low], self.in1, self.sem12.at[0], self.sem12.at[1],
                         {"dp": self.d + 1 - 2 * low})

    def two(self):
        high = self.d // 2
        return self.copy(self.half.at[1 - high], self.in2, self.sem12.at[2], self.sem12.at[3],
                         {"dp": self.d + 2 - 4 * high})

    def three(self, g, f):
        return self.copy(self.quarter.at[g], self.in3.at[f], self.s3.at[g], self.r3.at[f],
                         {"tm": g // self.spaces, "space": lax.rem(g, self.spaces)})

    def four(self, c, f):
        return self.copy(self.done.at[f], self.done.at[f], self.s4.at[c], self.r4.at[f],
                         {"dp": c})

    def first(self):
        _, group, rows, cols = self.part.shape
        split = self.grad.astype(BF16).reshape(group, 2, rows, cols)
        for h in range(2):
            self.part[h] = split[:, h]
        self.one().start()

    def second(self):
        self.one().wait_recv()
        total = self.part[lax.rem(self.d, 2)].astype(F32) + self.in1[...].astype(F32)
        cols = self.half.shape[-1]
        for h in range(2):
            self.half[h] = total[..., h * cols:(h + 1) * cols].astype(BF16)
        self.two().start()

    def third(self):
        self.two().wait_recv()
        total = self.half[self.d // 2].astype(F32) + self.in2[...].astype(F32)
        self.quarter[...] = total.astype(BF16)
        for g in self.members:
            self.three(g, self.me).start()
        self.in3[self.me] = self.quarter[self.me]

    def fourth(self):
        for g in self.members:
            self.three(g, g).wait_recv()
        self.done[self.d] = jnp.sum(self.in3[...].astype(F32), 0).astype(BF16)
        for c in self.others:
            self.four(c, self.d).start()

    def finish(self):
        for c in self.others:
            self.four(c, c).wait_recv()
        count, rows, cols = self.done.shape
        for c in range(count):
            self.out[pl.ds((c % 2) * rows, rows), pl.ds((c // 2) * cols, cols)] = self.done[c].astype(F32)
        self.one().wait_send()
        self.two().wait_send()
        for g in self.members:
            self.three(g, self.me).wait_send()
        for c in self.others:
            self.four(c, self.d).wait_send()


def sum_scratch(shape, group, clips):
    dma = pltpu.SemaphoreType.DMA
    rows, cols = shape[0] // group // 2, shape[1]
    return [
        pltpu.VMEM((2, group, rows, cols), BF16),
        pltpu.VMEM((group, rows, cols), BF16),
        pltpu.VMEM((2, group, rows, cols // 2), BF16),
        pltpu.VMEM((group, rows, cols // 2), BF16),
        pltpu.VMEM((group, rows, cols // 2), BF16),
        pltpu.VMEM((group, rows, cols // 2), BF16),
        pltpu.VMEM((clips, rows, cols // 2), BF16),
        dma((4,)),
        dma((group,)),
        dma((group,)),
        dma((clips,)),
        dma((clips,)),
    ]


def kernel(
    frames, spaces, clips, reduce, scale_mid, scale_top,
    feats, w_sp, w_tm, teach, w_dn, w_q, w_k, w_v, w_o, teach_top,
    student_out, gt_out, go_out,
    home, home_teach, home_top, v_sp, v_tm, v_dn, v_q, v_k, v_v, v_o,
    cells, edge_send, edges, edge_near, shifted, spat, turned, teacher, teacher_top, mid32, stu,
    in_sem, own_sem, fs, fr, es, er, ts, tr, ps, pr_, ss, sr, hs, hr,
    *sums,
):
    t = lax.axis_index("tm")
    s = lax.axis_index("space")
    rows, _, wc, chan = feats.shape
    half_rows, _, hc, width = teach_top.shape
    peers = [lax.rem(t + i, frames) for i in range(1, frames)]
    group = frames * spaces
    me = t * spaces + s
    members = [lax.rem(me + i, group) for i in range(1, group)]
    d = lax.axis_index("dp")
    others = [lax.rem(d + i, clips) for i in range(1, clips)]

    loads = [
        pltpu.make_async_copy(src, dst, in_sem.at[i])
        for i, (src, dst) in enumerate(
            ((feats, home), (w_sp, v_sp), (w_tm, v_tm), (w_dn, v_dn),
             (w_q, v_q), (w_k, v_k), (w_v, v_v), (w_o, v_o),
             (teach_top, home_top), (teach, home_teach))
        )
    ]
    for load in loads:
        load.start()
    own = [
        pltpu.make_async_copy(feats.at[:, t], cells.at[pl.ds(1, rows), t], own_sem.at[0]),
        pltpu.make_async_copy(teach.at[:, t], teacher.at[t], own_sem.at[1]),
        pltpu.make_async_copy(teach_top.at[:, t], teacher_top.at[t], own_sem.at[2]),
    ]
    for copy in own:
        copy.start()

    barrier = pltpu.get_barrier_semaphore()
    for g in members:
        pl.semaphore_signal(
            barrier, inc=1, device_id={"tm": g // spaces, "space": lax.rem(g, spaces)},
            device_id_type=MESH,
        )
    if reduce:
        for c in others:
            pl.semaphore_signal(barrier, inc=1, device_id={"dp": c}, device_id_type=MESH)

    loads[0].wait()
    for u in range(frames):
        if u > 0:
            left = home[:, u - 1, wc - 8:, :].astype(F32)[:, 7, :]
        else:
            left = jnp.zeros((rows, chan), F32)
        if u < frames - 1:
            right = home[:, u + 1, :8, :].astype(F32)[:, 0, :]
        else:
            right = jnp.zeros((rows, chan), F32)
        edge_send[u] = jnp.concatenate([left, right], 0).astype(BF16)

    pl.semaphore_wait(barrier, group - 1 + (clips - 1 if reduce else 0))

    def send(src, dst, ssem, rsem, u):
        return pltpu.make_async_remote_copy(
            src_ref=src, dst_ref=dst, send_sem=ssem, recv_sem=rsem,
            device_id={"tm": u}, device_id_type=MESH,
        )

    def feats_copy(u, f):
        return send(home.at[:, u], cells.at[pl.ds(1, rows), f], fs.at[u], fr.at[f], u)

    def edge_copy(u, f):
        return send(edge_send.at[u], edges.at[f], es.at[u], er.at[f], u)

    def teach_copy(u, f, h):
        part = pl.ds(h * (rows // 2), rows // 2)
        return send(home_teach.at[part, u], teacher.at[f, part],
                    ts.at[h * frames + u], tr.at[h * frames + f], u)

    def top_copy(u, f):
        return send(home_top.at[:, u], teacher_top.at[f], ps.at[u], pr_.at[f], u)

    def student_copy(u, f):
        return send(stu.at[u], student_out.at[:, f], ss.at[u], sr.at[f], u)

    for u in peers:
        edge_copy(u, t).start()
        feats_copy(u, t).start()
    edges[t] = edge_send[t]
    spat[pl.ds(0, 2)] = jnp.zeros((2,) + spat.shape[1:], BF16)

    @pl.when(s == 0)
    def _():
        cells[0] = jnp.zeros(cells.shape[1:], BF16)
        edge_near[0] = jnp.zeros(edges.shape, BF16)

    @pl.when(s == spaces - 1)
    def _():
        cells[rows + 1] = jnp.zeros(cells.shape[1:], BF16)
        edge_near[1] = jnp.zeros(edges.shape, BF16)

    own[0].wait()
    for f in peers:
        edge_copy(f, f).wait_recv()
        feats_copy(f, f).wait_recv()
    loads[8].wait()
    for u in peers:
        top_copy(u, t).start()
    loads[9].wait()
    for h in range(2):
        for u in peers:
            teach_copy(u, t, h).start()

    def halo(src, dst, i, j, to):
        return pltpu.make_async_remote_copy(
            src_ref=src, dst_ref=dst, send_sem=hs.at[i], recv_sem=hr.at[j],
            device_id={"space": to}, device_id_type=MESH,
        )

    def up(to):
        return (halo(cells.at[1], cells.at[rows + 1], 0, 0, to),
                halo(edges, edge_near.at[1], 1, 1, to))

    def down(to):
        return (halo(cells.at[rows], cells.at[0], 2, 2, to),
                halo(edges, edge_near.at[0], 3, 3, to))

    @pl.when(s > 0)
    def _():
        for copy in up(s - 1):
            copy.start()

    @pl.when(s < spaces - 1)
    def _():
        for copy in down(s + 1):
            copy.start()

    column = lax.broadcasted_iota(jnp.int32, (frames, wc, chan), 1)

    def shift(row, left, right):
        x = cells[row].astype(F32)
        a = jnp.where(column == 0, left, pltpu.roll(x, 1, 1))
        b = jnp.where(column == wc - 1, right, pltpu.roll(x, wc - 1, 1))
        flat = (frames * wc, chan)
        shifted[row, :, pl.ds(0, chan)] = a.astype(BF16).reshape(flat)
        shifted[row, :, pl.ds(chan, chan)] = cells[row].reshape(flat)
        shifted[row, :, pl.ds(2 * chan, chan)] = b.astype(BF16).reshape(flat)

    def conv(first, count):
        total = None
        for dy in range(3):
            block = shifted[pl.ds(first + dy, count)].reshape(count * frames * wc, 3 * chan)
            term = dot(block, v_sp[dy])
            total = term if total is None else total + term
        out = (total / (1.0 + jnp.exp(-total))).astype(BF16)
        out = out.reshape(count, frames, wc, chan)
        for i in range(count):
            spat[pl.ds(2, frames), first + i] = out[i]

    side = edges[...].astype(F32)
    for r in range(rows):
        shift(r + 1, side[:, r:r + 1, :], side[:, rows + r:rows + r + 1, :])
    loads[1].wait()
    conv(1, rows - 2)

    @pl.when(s < spaces - 1)
    def _():
        for copy in up(s + 1):
            copy.wait_recv()

    @pl.when(s > 0)
    def _():
        for copy in down(s - 1):
            copy.wait_recv()

    side = edge_near[0].astype(F32)
    shift(0, side[:, rows - 1:rows, :], side[:, 2 * rows - 1:2 * rows, :])
    side = edge_near[1].astype(F32)
    shift(rows + 1, side[:, 0:1, :], side[:, rows:rows + 1, :])
    conv(0, 1)
    conv(rows - 1, 1)

    loads[2].wait()
    half = chan // 2
    n = frames * rows * wc
    total = None
    for k in range(3):
        term = dot(spat[pl.ds(k, frames)].reshape(n, chan), v_tm[pl.ds(k * chan, chan), :])
        total = term if total is None else total + term
    for f in range(frames):
        base = cells[pl.ds(1, rows), f].astype(F32).reshape(rows * wc, chan)
        span = slice(f * rows * wc, (f + 1) * rows * wc)
        mid = (base + total[span]).astype(BF16).astype(F32)
        for h in range(2):
            mid32[h, span, :] = mid[:, h * half:(h + 1) * half]

    loads[3].wait()
    coarse = None
    count = frames * rows * wc // 2
    for b in range(2):
        part = jnp.concatenate(
            [mid32[h, pl.ds(b, count, stride=2), :] for h in range(2)], -1
        ).reshape(frames * half_rows, 2, hc, chan)
        for a in range(2):
            block = part[:, a].reshape(frames * half_rows * hc, chan).astype(BF16)
            term = dot(block, v_dn[a, b])
            coarse = term if coarse is None else coarse + term
    coarse = coarse.astype(BF16)

    for i in range(4, 8):
        loads[i].wait()
    points = half_rows * hc
    query = dot(coarse, v_q[...]).astype(BF16).astype(F32).reshape(frames, points, width)
    key = dot(coarse, v_k[...]).astype(BF16).astype(F32).reshape(frames, points, width)
    value = dot(coarse, v_v[...]).astype(BF16).astype(F32).reshape(frames, points, width)
    scale = 1.0 / math.sqrt(width)
    results = []
    for q in range(frames):
        score = [jnp.sum(query[q] * key[k], -1, keepdims=True) * scale for k in range(q + 1)]
        top = functools.reduce(jnp.maximum, score)
        weight = [jnp.exp(x - top) for x in score]
        total = functools.reduce(jnp.add, weight)
        acc = functools.reduce(jnp.add, [weight[k] * value[k] for k in range(q + 1)])
        results.append(acc / total)
    attended = jnp.concatenate(results, 0).astype(BF16)
    student = (coarse.astype(F32) + dot(attended, v_o[...])).astype(BF16)
    stu[...] = student.reshape(frames, half_rows, hc, width)
    keep = pltpu.make_async_copy(stu.at[t], student_out.at[:, t], own_sem.at[3])
    keep.start()


    turned_top = attended.T
    own[2].wait()
    for f in peers:
        top_copy(f, f).wait_recv()
    diff_top = (
        student.astype(F32) - teacher_top[...].astype(F32).reshape(frames * points, width)
    ).astype(BF16)
    grad_top = dot(turned_top, diff_top) * scale_top
    if reduce:
        top_sum = Sum(sums[12:], go_out, grad_top, d, me, members, others, spaces)
        top_sum.first()
    else:
        go_out[...] = grad_top

    low = rows // 2
    for h in range(2):
        for k in range(3):
            part = spat[pl.ds(k, frames), pl.ds(h * low, low)]
            turned[h, k] = part.reshape(n // 2, chan).T
    if reduce:
        top_sum.second()
    own[1].wait()
    grad = [None] * 3
    for h in range(2):
        for f in peers:
            teach_copy(f, f, h).wait_recv()
        if h == 1:
            for u in peers:
                student_copy(u, t).start()
        mid = jnp.concatenate(
            [mid32[i].reshape(frames, 2, low * wc, half)[:, h] for i in range(2)], -1
        ).reshape(n // 2, chan)
        diff = mid - teacher[:, pl.ds(h * low, low)].astype(F32).reshape(n // 2, chan)
        for k in range(3):
            term = dot(turned[h, k], diff.astype(BF16))
            grad[k] = term if h == 0 else grad[k] + term
        if reduce and h == 0:
            top_sum.third()
    grad = jnp.concatenate(grad, 0) * scale_mid
    if reduce:
        mid_sum = Sum(sums[:12], gt_out, grad, d, me, members, others, spaces)
        mid_sum.first()
        top_sum.fourth()
        mid_sum.second()
        mid_sum.third()
        top_sum.finish()
        mid_sum.fourth()
        mid_sum.finish()
    else:
        gt_out[...] = grad

    keep.wait()
    for u in peers:
        student_copy(u, u).wait_recv()
    for u in peers:
        edge_copy(u, t).wait_send()
        feats_copy(u, t).wait_send()
        for h in range(2):
            teach_copy(u, t, h).wait_send()
        top_copy(u, t).wait_send()
        student_copy(u, t).wait_send()

    @pl.when(s > 0)
    def _():
        for copy in up(s - 1):
            copy.wait_send()

    @pl.when(s < spaces - 1)
    def _():
        for copy in down(s + 1):
            copy.wait_send()


def hand_over(*refs):
    count = (len(refs) - 1) // 3
    ins, outs, held, sems = refs[:count], refs[count:2 * count], refs[2 * count:-1], refs[-1]
    reads = [pltpu.make_async_copy(ins[i], held[i], sems.at[0, i]) for i in range(count)]
    writes = [pltpu.make_async_copy(held[i], outs[i], sems.at[1, i]) for i in range(count)]
    for copy in reads:
        copy.start()
    for i in range(count):
        reads[i].wait()
        writes[i].start()
    for copy in writes:
        copy.wait()


def local(
    feats, w_spatial, w_temporal, teacher_mid, w_down, w_query, w_key, w_value, w_out, teacher_top
):
    frames = lax.axis_size("tm")
    spaces = lax.axis_size("space")
    devices_all = lax.axis_size("dp") * frames * spaces
    rows, cols, chan = feats.shape[2:]
    half_rows, half_cols, width = teacher_top.shape[2:]
    wc, hc = cols // frames, half_cols // frames
    scale_mid = 1.0 / math.sqrt(rows * cols * devices_all)
    scale_top = 1.0 / math.sqrt(half_rows * half_cols * devices_all)
    dma = pltpu.SemaphoreType.DMA
    group, clips = frames * spaces, lax.axis_size("dp")
    grads = (w_temporal.shape, w_out.shape)
    reduce = clips == 4 and all(r % (32 * group) == 0 and c % 256 == 0 for r, c in grads)
    pieces = [(r // group, c) if reduce else (r, c) for r, c in grads]
    student, gt, go = pl.pallas_call(
        functools.partial(kernel, frames, spaces, clips, reduce, scale_mid, scale_top),
        out_shape=(
            jax.ShapeDtypeStruct((half_rows, frames, hc, width), BF16),
            jax.ShapeDtypeStruct(pieces[0], F32),
            jax.ShapeDtypeStruct(pieces[1], F32),
        ),
        in_specs=[pl.BlockSpec(memory_space=pl.ANY)] * 10,
        out_specs=(pl.BlockSpec(memory_space=pltpu.VMEM),) * 3,
        scratch_shapes=[
            pltpu.VMEM((rows, frames, wc, chan), BF16),
            pltpu.VMEM((rows, frames, wc, chan), BF16),
            pltpu.VMEM((half_rows, frames, hc, width), BF16),
            pltpu.VMEM((3, 3 * chan, chan), BF16),
            pltpu.VMEM(w_temporal.shape, BF16),
            pltpu.VMEM(w_down.shape, BF16),
            pltpu.VMEM(w_query.shape, BF16),
            pltpu.VMEM(w_key.shape, BF16),
            pltpu.VMEM(w_value.shape, BF16),
            pltpu.VMEM(w_out.shape, BF16),
            pltpu.VMEM((rows + 2, frames, wc, chan), BF16),
            pltpu.VMEM((frames, 2 * rows, chan), BF16),
            pltpu.VMEM((frames, 2 * rows, chan), BF16),
            pltpu.VMEM((2, frames, 2 * rows, chan), BF16),
            pltpu.VMEM((rows + 2, frames * wc, 3 * chan), BF16),
            pltpu.VMEM((frames + 2, rows, wc, chan), BF16),
            pltpu.VMEM((2, 3, chan, frames * rows * wc // 2), BF16),
            pltpu.VMEM((frames, rows, wc, chan), BF16),
            pltpu.VMEM((frames, half_rows, hc, width), BF16),
            pltpu.VMEM((2, frames * rows * wc, chan // 2), F32),
            pltpu.VMEM((frames, half_rows, hc, width), BF16),
            dma((10,)),
            dma((4,)),
        ]
        + [dma((frames,))] * 4
        + [dma((2 * frames,))] * 2
        + [dma((frames,))] * 4
        + [dma((4,)), dma((4,))]
        + (sum_scratch(grads[0], group, clips) + sum_scratch(grads[1], group, clips) if reduce else []),
        compiler_params=pltpu.CompilerParams(
            collective_id=0, has_side_effects=True, vmem_limit_bytes=58 * 1024 * 1024
        ),
    )(
        feats.reshape(rows, frames, wc, chan),
        w_spatial.reshape(3, 3 * chan, chan),
        w_temporal,
        teacher_mid.reshape(rows, frames, wc, chan),
        w_down,
        w_query,
        w_key,
        w_value,
        w_out,
        teacher_top.reshape(half_rows, frames, hc, width),
    )
    if reduce:
        student, gt, go = pl.pallas_call(
            hand_over,
            out_shape=tuple(jax.ShapeDtypeStruct(x.shape, x.dtype) for x in (student, gt, go)),
            in_specs=[pl.BlockSpec(memory_space=pl.ANY)] * 3,
            out_specs=(pl.BlockSpec(memory_space=pl.ANY),) * 3,
            scratch_shapes=[pltpu.VMEM(x.shape, x.dtype) for x in (student, gt, go)]
            + [dma((2, 3))],
            compiler_params=pltpu.CompilerParams(vmem_limit_bytes=58 * 1024 * 1024),
        )(student, gt, go)
    else:
        gt = lax.psum_scatter(gt, ("tm", "space"), scatter_dimension=0, tiled=True)
        go = lax.psum_scatter(go, ("tm", "space"), scatter_dimension=0, tiled=True)
        gt, go = lax.psum((gt, go), "dp")
    return (student.reshape(1, 1, half_rows, half_cols, width), gt, go)


def solution(mesh):
    frame = P("dp", "tm", "space", None, None)
    return jax.shard_map(
        local,
        mesh=mesh,
        in_specs=(frame, P(), P(), frame, P(), P(), P(), P(), P(), frame),
        out_specs=(frame, P(("tm", "space"), None), P(("tm", "space"), None)),
        check_vma=False,
    )
```

```python
import functools
import math

import jax
import jax.numpy as jnp
from jax import lax
from jax.experimental import pallas as pl
from jax.experimental.pallas import tpu as pltpu
from jax.sharding import PartitionSpec as P

MESH = pl.DeviceIdType.MESH
F32 = jnp.float32
BF16 = jnp.bfloat16


def dot(a, b):
    return jnp.dot(a, b, preferred_element_type=F32)


class Sum:
    def __init__(self, refs, out, grad, d, me, members, others, spaces):
        (self.part, self.in1, self.half, self.in2, self.quarter, self.in3, self.done,
         self.sem12, self.s3, self.r3, self.s4, self.r4) = refs
        self.out, self.grad, self.d, self.me = out, grad, d, me
        self.members, self.others, self.spaces = members, others, spaces

    def copy(self, src, dst, ssem, rsem, to):
        return pltpu.make_async_remote_copy(
            src_ref=src, dst_ref=dst, send_sem=ssem, recv_sem=rsem,
            device_id=to, device_id_type=MESH,
        )

    def one(self):
        low = lax.rem(self.d, 2)
        return self.copy(self.part.at[1 - low], self.in1, self.sem12.at[0], self.sem12.at[1],
                         {"dp": self.d + 1 - 2 * low})

    def two(self):
        high = self.d // 2
        return self.copy(self.half.at[1 - high], self.in2, self.sem12.at[2], self.sem12.at[3],
                         {"dp": self.d + 2 - 4 * high})

    def three(self, g, f):
        return self.copy(self.quarter.at[g], self.in3.at[f], self.s3.at[g], self.r3.at[f],
                         {"tm": g // self.spaces, "space": lax.rem(g, self.spaces)})

    def four(self, c, f):
        return self.copy(self.done.at[f], self.done.at[f], self.s4.at[c], self.r4.at[f],
                         {"dp": c})

    def first(self):
        _, group, rows, cols = self.part.shape
        split = self.grad.astype(BF16).reshape(group, 2, rows, cols)
        for h in range(2):
            self.part[h] = split[:, h]
        self.one().start()

    def second(self):
        self.one().wait_recv()
        total = self.part[lax.rem(self.d, 2)].astype(F32) + self.in1[...].astype(F32)
        cols = self.half.shape[-1]
        for h in range(2):
            self.half[h] = total[..., h * cols:(h + 1) * cols].astype(BF16)
        self.two().start()

    def third(self):
        self.two().wait_recv()
        total = self.half[self.d // 2].astype(F32) + self.in2[...].astype(F32)
        self.quarter[...] = total.astype(BF16)
        for g in self.members:
            self.three(g, self.me).start()
        self.in3[self.me] = self.quarter[self.me]

    def fourth(self):
        for g in self.members:
            self.three(g, g).wait_recv()
        self.done[self.d] = jnp.sum(self.in3[...].astype(F32), 0).astype(BF16)
        for c in self.others:
            self.four(c, self.d).start()

    def finish(self):
        for c in self.others:
            self.four(c, c).wait_recv()
        count, rows, cols = self.done.shape
        for c in range(count):
            self.out[pl.ds((c % 2) * rows, rows), pl.ds((c // 2) * cols, cols)] = self.done[c].astype(F32)
        self.one().wait_send()
        self.two().wait_send()
        for g in self.members:
            self.three(g, self.me).wait_send()
        for c in self.others:
            self.four(c, self.d).wait_send()


def sum_scratch(shape, group, clips):
    dma = pltpu.SemaphoreType.DMA
    rows, cols = shape[0] // group // 2, shape[1]
    return [
        pltpu.VMEM((2, group, rows, cols), BF16),
        pltpu.VMEM((group, rows, cols), BF16),
        pltpu.VMEM((2, group, rows, cols // 2), BF16),
        pltpu.VMEM((group, rows, cols // 2), BF16),
        pltpu.VMEM((group, rows, cols // 2), BF16),
        pltpu.VMEM((group, rows, cols // 2), BF16),
        pltpu.VMEM((clips, rows, cols // 2), BF16),
        dma((4,)),
        dma((group,)),
        dma((group,)),
        dma((clips,)),
        dma((clips,)),
    ]


def kernel(
    frames, spaces, clips, reduce, scale_mid, scale_top,
    feats, w_sp, w_tm, teach, w_dn, w_q, w_k, w_v, w_o, teach_top,
    student_out, gt_out, go_out,
    home, home_teach, v_sp, v_tm, v_dn, v_q, v_k, v_v, v_o,
    cells, edge_send, edges, edge_near, shifted, spat, turned, teacher, teacher_top, mid32, stu,
    in_sem, own_sem, fs, fr, es, er, ts, tr, ps, pr_, ss, sr, hs, hr,
    *sums,
):
    t = lax.axis_index("tm")
    s = lax.axis_index("space")
    rows, _, wc, chan = feats.shape
    half_rows, _, hc, width = teach_top.shape
    peers = [lax.rem(t + i, frames) for i in range(1, frames)]
    group = frames * spaces
    me = t * spaces + s
    members = [lax.rem(me + i, group) for i in range(1, group)]
    d = lax.axis_index("dp")
    others = [lax.rem(d + i, clips) for i in range(1, clips)]

    loads = [
        pltpu.make_async_copy(src, dst, in_sem.at[i])
        for i, (src, dst) in enumerate(
            ((feats, home), (w_sp, v_sp), (w_tm, v_tm), (w_dn, v_dn),
             (w_q, v_q), (w_k, v_k), (w_v, v_v), (w_o, v_o),
             (teach, home_teach))
        )
    ]
    own = [
        pltpu.make_async_copy(feats.at[:, t], cells.at[pl.ds(1, rows), t], own_sem.at[0]),
        pltpu.make_async_copy(teach.at[:, t], teacher.at[t], own_sem.at[1]),
        pltpu.make_async_copy(teach_top.at[:, t], teacher_top.at[t], own_sem.at[2]),
    ]
    barrier = pltpu.get_barrier_semaphore()
    for g in members:
        pl.semaphore_signal(
            barrier, inc=1, device_id={"tm": g // spaces, "space": lax.rem(g, spaces)},
            device_id_type=MESH,
        )
    if reduce:
        for c in others:
            pl.semaphore_signal(barrier, inc=1, device_id={"dp": c}, device_id_type=MESH)

    loads[0].start()

    def send(src, dst, ssem, rsem, u):
        return pltpu.make_async_remote_copy(
            src_ref=src, dst_ref=dst, send_sem=ssem, recv_sem=rsem,
            device_id={"tm": u}, device_id_type=MESH,
        )

    def feats_copy(u, f):
        return send(feats.at[:, u], cells.at[pl.ds(1, rows), f], fs.at[u], fr.at[f], u)

    def edge_copy(u, f):
        return send(edge_send.at[u], edges.at[f], es.at[u], er.at[f], u)

    def teach_copy(u, f, h):
        part = pl.ds(h * (rows // 2), rows // 2)
        return send(home_teach.at[part, u], teacher.at[f, part],
                    ts.at[h * frames + u], tr.at[h * frames + f], u)

    def top_copy(u, f):
        return send(teach_top.at[:, u], teacher_top.at[f], ps.at[u], pr_.at[f], u)

    def student_copy(u, f):
        return send(stu.at[u], student_out.at[:, f], ss.at[u], sr.at[f], u)

    pl.semaphore_wait(barrier, group - 1 + (clips - 1 if reduce else 0))
    for u in peers:
        feats_copy(u, t).start()
    for copy in own:
        copy.start()
    for load in loads[1:]:
        load.start()

    loads[0].wait()
    for u in range(frames):
        if u > 0:
            left = home[:, u - 1, wc - 8:, :].astype(F32)[:, 7, :]
        else:
            left = jnp.zeros((rows, chan), F32)
        if u < frames - 1:
            right = home[:, u + 1, :8, :].astype(F32)[:, 0, :]
        else:
            right = jnp.zeros((rows, chan), F32)
        edge_send[u] = jnp.concatenate([left, right], 0).astype(BF16)

    for u in peers:
        edge_copy(u, t).start()
    for u in peers:
        top_copy(u, t).start()
    edges[t] = edge_send[t]
    spat[pl.ds(0, 2)] = jnp.zeros((2,) + spat.shape[1:], BF16)

    @pl.when(s == 0)
    def _():
        cells[0] = jnp.zeros(cells.shape[1:], BF16)
        edge_near[0] = jnp.zeros(edges.shape, BF16)

    @pl.when(s == spaces - 1)
    def _():
        cells[rows + 1] = jnp.zeros(cells.shape[1:], BF16)
        edge_near[1] = jnp.zeros(edges.shape, BF16)

    own[0].wait()
    for f in peers:
        edge_copy(f, f).wait_recv()
        feats_copy(f, f).wait_recv()
    loads[8].wait()
    for h in range(2):
        for u in peers:
            teach_copy(u, t, h).start()

    def halo(src, dst, i, j, to):
        return pltpu.make_async_remote_copy(
            src_ref=src, dst_ref=dst, send_sem=hs.at[i], recv_sem=hr.at[j],
            device_id={"space": to}, device_id_type=MESH,
        )

    def up(to):
        return (halo(cells.at[1], cells.at[rows + 1], 0, 0, to),
                halo(edges, edge_near.at[1], 1, 1, to))

    def down(to):
        return (halo(cells.at[rows], cells.at[0], 2, 2, to),
                halo(edges, edge_near.at[0], 3, 3, to))

    @pl.when(s > 0)
    def _():
        for copy in up(s - 1):
            copy.start()

    @pl.when(s < spaces - 1)
    def _():
        for copy in down(s + 1):
            copy.start()

    column = lax.broadcasted_iota(jnp.int32, (frames, wc, chan), 1)

    def shift(row, left, right):
        x = cells[row].astype(F32)
        a = jnp.where(column == 0, left, pltpu.roll(x, 1, 1))
        b = jnp.where(column == wc - 1, right, pltpu.roll(x, wc - 1, 1))
        flat = (frames * wc, chan)
        shifted[row, :, pl.ds(0, chan)] = a.astype(BF16).reshape(flat)
        shifted[row, :, pl.ds(chan, chan)] = cells[row].reshape(flat)
        shifted[row, :, pl.ds(2 * chan, chan)] = b.astype(BF16).reshape(flat)

    def conv(first, count):
        total = None
        for dy in range(3):
            block = shifted[pl.ds(first + dy, count)].reshape(count * frames * wc, 3 * chan)
            term = dot(block, v_sp[dy])
            total = term if total is None else total + term
        out = (total / (1.0 + jnp.exp(-total))).astype(BF16)
        out = out.reshape(count, frames, wc, chan)
        for i in range(count):
            spat[pl.ds(2, frames), first + i] = out[i]

    side = edges[...].astype(F32)
    for r in range(rows):
        shift(r + 1, side[:, r:r + 1, :], side[:, rows + r:rows + r + 1, :])
    loads[1].wait()
    conv(1, rows - 2)

    @pl.when(s < spaces - 1)
    def _():
        for copy in up(s + 1):
            copy.wait_recv()

    @pl.when(s > 0)
    def _():
        for copy in down(s - 1):
            copy.wait_recv()

    side = edge_near[0].astype(F32)
    shift(0, side[:, rows - 1:rows, :], side[:, 2 * rows - 1:2 * rows, :])
    side = edge_near[1].astype(F32)
    shift(rows + 1, side[:, 0:1, :], side[:, rows:rows + 1, :])
    conv(0, 1)
    conv(rows - 1, 1)

    loads[2].wait()
    half = chan // 2
    n = frames * rows * wc
    total = None
    for k in range(3):
        term = dot(spat[pl.ds(k, frames)].reshape(n, chan), v_tm[pl.ds(k * chan, chan), :])
        total = term if total is None else total + term
    for f in range(frames):
        base = cells[pl.ds(1, rows), f].astype(F32).reshape(rows * wc, chan)
        span = slice(f * rows * wc, (f + 1) * rows * wc)
        mid = (base + total[span]).astype(BF16).astype(F32)
        for h in range(2):
            mid32[h, span, :] = mid[:, h * half:(h + 1) * half]

    loads[3].wait()
    coarse = None
    count = frames * rows * wc // 2
    for b in range(2):
        part = jnp.concatenate(
            [mid32[h, pl.ds(b, count, stride=2), :] for h in range(2)], -1
        ).reshape(frames * half_rows, 2, hc, chan)
        for a in range(2):
            block = part[:, a].reshape(frames * half_rows * hc, chan).astype(BF16)
            term = dot(block, v_dn[a, b])
            coarse = term if coarse is None else coarse + term
    coarse = coarse.astype(BF16)

    for i in range(4, 8):
        loads[i].wait()
    points = half_rows * hc
    query = dot(coarse, v_q[...]).astype(BF16).astype(F32).reshape(frames, points, width)
    key = dot(coarse, v_k[...]).astype(BF16).astype(F32).reshape(frames, points, width)
    value = dot(coarse, v_v[...]).astype(BF16).astype(F32).reshape(frames, points, width)
    scale = 1.0 / math.sqrt(width)
    results = []
    for q in range(frames):
        score = [jnp.sum(query[q] * key[k], -1, keepdims=True) * scale for k in range(q + 1)]
        top = functools.reduce(jnp.maximum, score)
        weight = [jnp.exp(x - top) for x in score]
        total = functools.reduce(jnp.add, weight)
        acc = functools.reduce(jnp.add, [weight[k] * value[k] for k in range(q + 1)])
        results.append(acc / total)
    attended = jnp.concatenate(results, 0).astype(BF16)
    student = (coarse.astype(F32) + dot(attended, v_o[...])).astype(BF16)
    stu[...] = student.reshape(frames, half_rows, hc, width)
    keep = pltpu.make_async_copy(stu.at[t], student_out.at[:, t], own_sem.at[3])
    keep.start()


    turned_top = attended.T
    own[2].wait()
    for f in peers:
        top_copy(f, f).wait_recv()
    diff_top = (
        student.astype(F32) - teacher_top[...].astype(F32).reshape(frames * points, width)
    ).astype(BF16)
    grad_top = dot(turned_top, diff_top) * scale_top
    if reduce:
        top_sum = Sum(sums[12:], go_out, grad_top, d, me, members, others, spaces)
        top_sum.first()
    else:
        go_out[...] = grad_top

    low = rows // 2
    for h in range(2):
        for k in range(3):
            part = spat[pl.ds(k, frames), pl.ds(h * low, low)]
            turned[h, k] = part.reshape(n // 2, chan).T
    if reduce:
        top_sum.second()
    own[1].wait()
    grad = [None] * 3
    for h in range(2):
        for f in peers:
            teach_copy(f, f, h).wait_recv()
        if h == 1:
            for u in peers:
                student_copy(u, t).start()
        mid = jnp.concatenate(
            [mid32[i].reshape(frames, 2, low * wc, half)[:, h] for i in range(2)], -1
        ).reshape(n // 2, chan)
        diff = mid - teacher[:, pl.ds(h * low, low)].astype(F32).reshape(n // 2, chan)
        for k in range(3):
            term = dot(turned[h, k], diff.astype(BF16))
            grad[k] = term if h == 0 else grad[k] + term
        if reduce and h == 0:
            top_sum.third()
    grad = jnp.concatenate(grad, 0) * scale_mid
    if reduce:
        mid_sum = Sum(sums[:12], gt_out, grad, d, me, members, others, spaces)
        mid_sum.first()
        top_sum.fourth()
        mid_sum.second()
        mid_sum.third()
        top_sum.finish()
        mid_sum.fourth()
        mid_sum.finish()
    else:
        gt_out[...] = grad

    keep.wait()
    for u in peers:
        student_copy(u, u).wait_recv()
    for u in peers:
        edge_copy(u, t).wait_send()
        feats_copy(u, t).wait_send()
        for h in range(2):
            teach_copy(u, t, h).wait_send()
        top_copy(u, t).wait_send()
        student_copy(u, t).wait_send()

    @pl.when(s > 0)
    def _():
        for copy in up(s - 1):
            copy.wait_send()

    @pl.when(s < spaces - 1)
    def _():
        for copy in down(s + 1):
            copy.wait_send()


def hand_over(*refs):
    count = (len(refs) - 1) // 3
    ins, outs, held, sems = refs[:count], refs[count:2 * count], refs[2 * count:-1], refs[-1]
    reads = [pltpu.make_async_copy(ins[i], held[i], sems.at[0, i]) for i in range(count)]
    writes = [pltpu.make_async_copy(held[i], outs[i], sems.at[1, i]) for i in range(count)]
    for copy in reads:
        copy.start()
    for i in range(count):
        reads[i].wait()
        writes[i].start()
    for copy in writes:
        copy.wait()


def local(
    feats, w_spatial, w_temporal, teacher_mid, w_down, w_query, w_key, w_value, w_out, teacher_top
):
    frames = lax.axis_size("tm")
    spaces = lax.axis_size("space")
    devices_all = lax.axis_size("dp") * frames * spaces
    rows, cols, chan = feats.shape[2:]
    half_rows, half_cols, width = teacher_top.shape[2:]
    wc, hc = cols // frames, half_cols // frames
    scale_mid = 1.0 / math.sqrt(rows * cols * devices_all)
    scale_top = 1.0 / math.sqrt(half_rows * half_cols * devices_all)
    dma = pltpu.SemaphoreType.DMA
    group, clips = frames * spaces, lax.axis_size("dp")
    grads = (w_temporal.shape, w_out.shape)
    reduce = clips == 4 and all(r % (32 * group) == 0 and c % 256 == 0 for r, c in grads)
    pieces = [(r // group, c) if reduce else (r, c) for r, c in grads]
    student, gt, go = pl.pallas_call(
        functools.partial(kernel, frames, spaces, clips, reduce, scale_mid, scale_top),
        out_shape=(
            jax.ShapeDtypeStruct((half_rows, frames, hc, width), BF16),
            jax.ShapeDtypeStruct(pieces[0], F32),
            jax.ShapeDtypeStruct(pieces[1], F32),
        ),
        in_specs=[pl.BlockSpec(memory_space=pl.ANY)] * 10,
        out_specs=(pl.BlockSpec(memory_space=pltpu.VMEM),) * 3,
        scratch_shapes=[
            pltpu.VMEM((rows, frames, wc, chan), BF16),
            pltpu.VMEM((rows, frames, wc, chan), BF16),
            pltpu.VMEM((3, 3 * chan, chan), BF16),
            pltpu.VMEM(w_temporal.shape, BF16),
            pltpu.VMEM(w_down.shape, BF16),
            pltpu.VMEM(w_query.shape, BF16),
            pltpu.VMEM(w_key.shape, BF16),
            pltpu.VMEM(w_value.shape, BF16),
            pltpu.VMEM(w_out.shape, BF16),
            pltpu.VMEM((rows + 2, frames, wc, chan), BF16),
            pltpu.VMEM((frames, 2 * rows, chan), BF16),
            pltpu.VMEM((frames, 2 * rows, chan), BF16),
            pltpu.VMEM((2, frames, 2 * rows, chan), BF16),
            pltpu.VMEM((rows + 2, frames * wc, 3 * chan), BF16),
            pltpu.VMEM((frames + 2, rows, wc, chan), BF16),
            pltpu.VMEM((2, 3, chan, frames * rows * wc // 2), BF16),
            pltpu.VMEM((frames, rows, wc, chan), BF16),
            pltpu.VMEM((frames, half_rows, hc, width), BF16),
            pltpu.VMEM((2, frames * rows * wc, chan // 2), F32),
            pltpu.VMEM((frames, half_rows, hc, width), BF16),
            dma((9,)),
            dma((4,)),
        ]
        + [dma((frames,))] * 4
        + [dma((2 * frames,))] * 2
        + [dma((frames,))] * 4
        + [dma((4,)), dma((4,))]
        + (sum_scratch(grads[0], group, clips) + sum_scratch(grads[1], group, clips) if reduce else []),
        compiler_params=pltpu.CompilerParams(
            collective_id=0, has_side_effects=True, vmem_limit_bytes=58 * 1024 * 1024
        ),
    )(
        feats.reshape(rows, frames, wc, chan),
        w_spatial.reshape(3, 3 * chan, chan),
        w_temporal,
        teacher_mid.reshape(rows, frames, wc, chan),
        w_down,
        w_query,
        w_key,
        w_value,
        w_out,
        teacher_top.reshape(half_rows, frames, hc, width),
    )
    if reduce:
        student, gt, go = pl.pallas_call(
            hand_over,
            out_shape=tuple(jax.ShapeDtypeStruct(x.shape, x.dtype) for x in (student, gt, go)),
            in_specs=[pl.BlockSpec(memory_space=pl.ANY)] * 3,
            out_specs=(pl.BlockSpec(memory_space=pl.ANY),) * 3,
            scratch_shapes=[pltpu.VMEM(x.shape, x.dtype) for x in (student, gt, go)]
            + [dma((2, 3))],
            compiler_params=pltpu.CompilerParams(vmem_limit_bytes=58 * 1024 * 1024),
        )(student, gt, go)
    else:
        gt = lax.psum_scatter(gt, ("tm", "space"), scatter_dimension=0, tiled=True)
        go = lax.psum_scatter(go, ("tm", "space"), scatter_dimension=0, tiled=True)
        gt, go = lax.psum((gt, go), "dp")
    return (student.reshape(1, 1, half_rows, half_cols, width), gt, go)


def solution(mesh):
    frame = P("dp", "tm", "space", None, None)
    return jax.shard_map(
        local,
        mesh=mesh,
        in_specs=(frame, P(), P(), frame, P(), P(), P(), P(), P(), frame),
        out_specs=(frame, P(("tm", "space"), None), P(("tm", "space"), None)),
        check_vma=False,
    )
```

```python
import functools
import math

import jax
import jax.numpy as jnp
from jax import lax
from jax.experimental import pallas as pl
from jax.experimental.pallas import tpu as pltpu
from jax.sharding import PartitionSpec as P

MESH = pl.DeviceIdType.MESH
F32 = jnp.float32
BF16 = jnp.bfloat16


def dot(a, b):
    return jnp.dot(a, b, preferred_element_type=F32)


class Sum:
    def __init__(self, refs, out, grad, d, me, members, others, spaces):
        (self.part, self.in1, self.half, self.in2, self.quarter, self.in3, self.done,
         self.sem12, self.s3, self.r3, self.s4, self.r4) = refs
        self.out, self.grad, self.d, self.me = out, grad, d, me
        self.members, self.others, self.spaces = members, others, spaces

    def copy(self, src, dst, ssem, rsem, to):
        return pltpu.make_async_remote_copy(
            src_ref=src, dst_ref=dst, send_sem=ssem, recv_sem=rsem,
            device_id=to, device_id_type=MESH,
        )

    def one(self):
        low = lax.rem(self.d, 2)
        return self.copy(self.part.at[1 - low], self.in1, self.sem12.at[0], self.sem12.at[1],
                         {"dp": self.d + 1 - 2 * low})

    def two(self):
        high = self.d // 2
        return self.copy(self.half.at[1 - high], self.in2, self.sem12.at[2], self.sem12.at[3],
                         {"dp": self.d + 2 - 4 * high})

    def three(self, g, f):
        return self.copy(self.quarter.at[g], self.in3.at[f], self.s3.at[g], self.r3.at[f],
                         {"tm": g // self.spaces, "space": lax.rem(g, self.spaces)})

    def four(self, c, f):
        return self.copy(self.done.at[f], self.done.at[f], self.s4.at[c], self.r4.at[f],
                         {"dp": c})

    def first(self):
        _, group, rows, cols = self.part.shape
        split = self.grad.astype(BF16).reshape(group, 2, rows, cols)
        for h in range(2):
            self.part[h] = split[:, h]
        self.one().start()

    def second(self):
        self.one().wait_recv()
        total = self.part[lax.rem(self.d, 2)].astype(F32) + self.in1[...].astype(F32)
        cols = self.half.shape[-1]
        for h in range(2):
            self.half[h] = total[..., h * cols:(h + 1) * cols].astype(BF16)
        self.two().start()

    def third(self):
        self.two().wait_recv()
        total = self.half[self.d // 2].astype(F32) + self.in2[...].astype(F32)
        self.quarter[...] = total.astype(BF16)
        for g in self.members:
            self.three(g, self.me).start()
        self.in3[self.me] = self.quarter[self.me]

    def fourth(self):
        for g in self.members:
            self.three(g, g).wait_recv()
        self.done[self.d] = jnp.sum(self.in3[...].astype(F32), 0).astype(BF16)
        for c in self.others:
            self.four(c, self.d).start()

    def finish(self):
        for c in self.others:
            self.four(c, c).wait_recv()
        count, rows, cols = self.done.shape
        for c in range(count):
            self.out[pl.ds((c % 2) * rows, rows), pl.ds((c // 2) * cols, cols)] = self.done[c].astype(F32)
        self.one().wait_send()
        self.two().wait_send()
        for g in self.members:
            self.three(g, self.me).wait_send()
        for c in self.others:
            self.four(c, self.d).wait_send()


def sum_scratch(shape, group, clips):
    dma = pltpu.SemaphoreType.DMA
    rows, cols = shape[0] // group // 2, shape[1]
    return [
        pltpu.VMEM((2, group, rows, cols), BF16),
        pltpu.VMEM((group, rows, cols), BF16),
        pltpu.VMEM((2, group, rows, cols // 2), BF16),
        pltpu.VMEM((group, rows, cols // 2), BF16),
        pltpu.VMEM((group, rows, cols // 2), BF16),
        pltpu.VMEM((group, rows, cols // 2), BF16),
        pltpu.VMEM((clips, rows, cols // 2), BF16),
        dma((4,)),
        dma((group,)),
        dma((group,)),
        dma((clips,)),
        dma((clips,)),
    ]


def kernel(
    frames, spaces, clips, reduce, scale_mid, scale_top,
    feats, w_sp, w_tm, teach, w_dn, w_q, w_k, w_v, w_o, teach_top,
    student_out, gt_out, go_out,
    home, v_sp, v_tm, v_dn, v_q, v_k, v_v, v_o,
    cells, edge_send, edges, edge_near, shifted, spat, turned, teacher, teacher_top, mid32, stu,
    in_sem, own_sem, fs, fr, es, er, ts, tr, ps, pr_, ss, sr, hs, hr,
    *sums,
):
    t = lax.axis_index("tm")
    s = lax.axis_index("space")
    rows, _, wc, chan = feats.shape
    half_rows, _, hc, width = teach_top.shape
    peers = [lax.rem(t + i, frames) for i in range(1, frames)]
    group = frames * spaces
    me = t * spaces + s
    members = [lax.rem(me + i, group) for i in range(1, group)]
    d = lax.axis_index("dp")
    others = [lax.rem(d + i, clips) for i in range(1, clips)]

    loads = [
        pltpu.make_async_copy(src, dst, in_sem.at[i])
        for i, (src, dst) in enumerate(
            ((feats, home), (w_sp, v_sp), (w_tm, v_tm), (w_dn, v_dn),
             (w_q, v_q), (w_k, v_k), (w_v, v_v), (w_o, v_o))
        )
    ]
    own = [
        pltpu.make_async_copy(feats.at[:, t], cells.at[pl.ds(1, rows), t], own_sem.at[0]),
        pltpu.make_async_copy(teach.at[:, t], teacher.at[t], own_sem.at[1]),
        pltpu.make_async_copy(teach_top.at[:, t], teacher_top.at[t], own_sem.at[2]),
    ]
    barrier = pltpu.get_barrier_semaphore()
    for g in members:
        pl.semaphore_signal(
            barrier, inc=1, device_id={"tm": g // spaces, "space": lax.rem(g, spaces)},
            device_id_type=MESH,
        )
    if reduce:
        for c in others:
            pl.semaphore_signal(barrier, inc=1, device_id={"dp": c}, device_id_type=MESH)

    loads[0].start()

    def send(src, dst, ssem, rsem, u):
        return pltpu.make_async_remote_copy(
            src_ref=src, dst_ref=dst, send_sem=ssem, recv_sem=rsem,
            device_id={"tm": u}, device_id_type=MESH,
        )

    def feats_copy(u, f):
        return send(feats.at[:, u], cells.at[pl.ds(1, rows), f], fs.at[u], fr.at[f], u)

    def edge_copy(u, f):
        return send(edge_send.at[u], edges.at[f], es.at[u], er.at[f], u)

    def teach_copy(u, f):
        return send(teach.at[:, u], teacher.at[f], ts.at[u], tr.at[f], u)

    def top_copy(u, f):
        return send(teach_top.at[:, u], teacher_top.at[f], ps.at[u], pr_.at[f], u)

    def student_copy(u, f):
        return send(stu.at[u], student_out.at[:, f], ss.at[u], sr.at[f], u)

    pl.semaphore_wait(barrier, group - 1 + (clips - 1 if reduce else 0))
    for u in peers:
        feats_copy(u, t).start()
    for copy in own:
        copy.start()
    for load in loads[1:]:
        load.start()

    loads[0].wait()
    for u in range(frames):
        if u > 0:
            left = home[:, u - 1, wc - 8:, :].astype(F32)[:, 7, :]
        else:
            left = jnp.zeros((rows, chan), F32)
        if u < frames - 1:
            right = home[:, u + 1, :8, :].astype(F32)[:, 0, :]
        else:
            right = jnp.zeros((rows, chan), F32)
        edge_send[u] = jnp.concatenate([left, right], 0).astype(BF16)

    for u in peers:
        edge_copy(u, t).start()
    edges[t] = edge_send[t]
    spat[pl.ds(0, 2)] = jnp.zeros((2,) + spat.shape[1:], BF16)

    @pl.when(s == 0)
    def _():
        cells[0] = jnp.zeros(cells.shape[1:], BF16)
        edge_near[0] = jnp.zeros(edges.shape, BF16)

    @pl.when(s == spaces - 1)
    def _():
        cells[rows + 1] = jnp.zeros(cells.shape[1:], BF16)
        edge_near[1] = jnp.zeros(edges.shape, BF16)

    own[0].wait()
    for f in peers:
        edge_copy(f, f).wait_recv()
        feats_copy(f, f).wait_recv()
    for u in peers:
        top_copy(u, t).start()
    for u in peers:
        teach_copy(u, t).start()

    def halo(src, dst, i, j, to):
        return pltpu.make_async_remote_copy(
            src_ref=src, dst_ref=dst, send_sem=hs.at[i], recv_sem=hr.at[j],
            device_id={"space": to}, device_id_type=MESH,
        )

    def up(to):
        return (halo(cells.at[1], cells.at[rows + 1], 0, 0, to),
                halo(edges, edge_near.at[1], 1, 1, to))

    def down(to):
        return (halo(cells.at[rows], cells.at[0], 2, 2, to),
                halo(edges, edge_near.at[0], 3, 3, to))

    @pl.when(s > 0)
    def _():
        for copy in up(s - 1):
            copy.start()

    @pl.when(s < spaces - 1)
    def _():
        for copy in down(s + 1):
            copy.start()

    column = lax.broadcasted_iota(jnp.int32, (frames, wc, chan), 1)

    def shift(row, left, right):
        x = cells[row].astype(F32)
        a = jnp.where(column == 0, left, pltpu.roll(x, 1, 1))
        b = jnp.where(column == wc - 1, right, pltpu.roll(x, wc - 1, 1))
        flat = (frames * wc, chan)
        shifted[row, :, pl.ds(0, chan)] = a.astype(BF16).reshape(flat)
        shifted[row, :, pl.ds(chan, chan)] = cells[row].reshape(flat)
        shifted[row, :, pl.ds(2 * chan, chan)] = b.astype(BF16).reshape(flat)

    def conv(spans):
        count = sum(c for _, c in spans)
        total = None
        for dy in range(3):
            blocks = [
                shifted[pl.ds(first + dy, c)].reshape(c * frames * wc, 3 * chan)
                for first, c in spans
            ]
            block = blocks[0] if len(blocks) == 1 else jnp.concatenate(blocks, 0)
            term = dot(block, v_sp[dy])
            total = term if total is None else total + term
        out = (total / (1.0 + jnp.exp(-total))).astype(BF16)
        out = out.reshape(count, frames, wc, chan)
        places = [first + i for first, c in spans for i in range(c)]
        for i, row in enumerate(places):
            spat[pl.ds(2, frames), row] = out[i]

    side = edges[...].astype(F32)
    for r in range(rows):
        shift(r + 1, side[:, r:r + 1, :], side[:, rows + r:rows + r + 1, :])
    loads[1].wait()
    conv([(1, rows - 2)])

    @pl.when(s < spaces - 1)
    def _():
        for copy in up(s + 1):
            copy.wait_recv()

    @pl.when(s > 0)
    def _():
        for copy in down(s - 1):
            copy.wait_recv()

    side = edge_near[0].astype(F32)
    shift(0, side[:, rows - 1:rows, :], side[:, 2 * rows - 1:2 * rows, :])
    side = edge_near[1].astype(F32)
    shift(rows + 1, side[:, 0:1, :], side[:, rows:rows + 1, :])
    conv([(0, 1), (rows - 1, 1)])

    loads[2].wait()
    half = chan // 2
    n = frames * rows * wc
    total = None
    for k in range(3):
        term = dot(spat[pl.ds(k, frames)].reshape(n, chan), v_tm[pl.ds(k * chan, chan), :])
        total = term if total is None else total + term
    for f in range(frames):
        base = cells[pl.ds(1, rows), f].astype(F32).reshape(rows * wc, chan)
        span = slice(f * rows * wc, (f + 1) * rows * wc)
        mid = (base + total[span]).astype(BF16).astype(F32)
        for h in range(2):
            mid32[h, span, :] = mid[:, h * half:(h + 1) * half]

    loads[3].wait()
    coarse = None
    count = frames * rows * wc // 2
    for b in range(2):
        part = jnp.concatenate(
            [mid32[h, pl.ds(b, count, stride=2), :] for h in range(2)], -1
        ).reshape(frames * half_rows, 2, hc, chan)
        for a in range(2):
            block = part[:, a].reshape(frames * half_rows * hc, chan).astype(BF16)
            term = dot(block, v_dn[a, b])
            coarse = term if coarse is None else coarse + term
    coarse = coarse.astype(BF16)

    for i in range(4, 8):
        loads[i].wait()
    points = half_rows * hc
    query = dot(coarse, v_q[...]).astype(BF16).astype(F32).reshape(frames, points, width)
    key = dot(coarse, v_k[...]).astype(BF16).astype(F32).reshape(frames, points, width)
    value = dot(coarse, v_v[...]).astype(BF16).astype(F32).reshape(frames, points, width)
    scale = 1.0 / math.sqrt(width)
    results = []
    for q in range(frames):
        score = [jnp.sum(query[q] * key[k], -1, keepdims=True) * scale for k in range(q + 1)]
        top = functools.reduce(jnp.maximum, score)
        weight = [jnp.exp(x - top) for x in score]
        total = functools.reduce(jnp.add, weight)
        acc = functools.reduce(jnp.add, [weight[k] * value[k] for k in range(q + 1)])
        results.append(acc / total)
    attended = jnp.concatenate(results, 0).astype(BF16)
    student = (coarse.astype(F32) + dot(attended, v_o[...])).astype(BF16)
    stu[...] = student.reshape(frames, half_rows, hc, width)
    keep = pltpu.make_async_copy(stu.at[t], student_out.at[:, t], own_sem.at[3])
    keep.start()


    turned_top = attended.T
    own[2].wait()
    for f in peers:
        top_copy(f, f).wait_recv()
    diff_top = (
        student.astype(F32) - teacher_top[...].astype(F32).reshape(frames * points, width)
    ).astype(BF16)
    grad_top = dot(turned_top, diff_top) * scale_top
    if reduce:
        top_sum = Sum(sums[12:], go_out, grad_top, d, me, members, others, spaces)
        top_sum.first()
    else:
        go_out[...] = grad_top

    frame = rows * wc
    turned[:, pl.ds(0, 2 * frame)] = jnp.zeros((chan, 2 * frame), BF16)
    for f in range(frames):
        turned[:, pl.ds((f + 2) * frame, frame)] = spat[f + 2].reshape(frame, chan).T
    if reduce:
        top_sum.second()
    own[1].wait()
    for f in peers:
        teach_copy(f, f).wait_recv()
    for u in peers:
        student_copy(u, t).start()
    mid = jnp.concatenate([mid32[0], mid32[1]], -1)
    diff = (mid - teacher[...].astype(F32).reshape(n, chan)).astype(BF16)
    grad = [dot(turned[:, pl.ds(k * frame, n)], diff) for k in range(3)]
    grad = jnp.concatenate(grad, 0) * scale_mid
    if reduce:
        mid_sum = Sum(sums[:12], gt_out, grad, d, me, members, others, spaces)
        mid_sum.first()
        top_sum.third()
        mid_sum.second()
        top_sum.fourth()
        mid_sum.third()
        top_sum.finish()
        mid_sum.fourth()
        mid_sum.finish()
    else:
        gt_out[...] = grad

    keep.wait()
    for u in peers:
        student_copy(u, u).wait_recv()
    for u in peers:
        edge_copy(u, t).wait_send()
        feats_copy(u, t).wait_send()
        teach_copy(u, t).wait_send()
        top_copy(u, t).wait_send()
        student_copy(u, t).wait_send()

    @pl.when(s > 0)
    def _():
        for copy in up(s - 1):
            copy.wait_send()

    @pl.when(s < spaces - 1)
    def _():
        for copy in down(s + 1):
            copy.wait_send()


def hand_over(*refs):
    count = (len(refs) - 1) // 3
    ins, outs, held, sems = refs[:count], refs[count:2 * count], refs[2 * count:-1], refs[-1]
    reads = [pltpu.make_async_copy(ins[i], held[i], sems.at[0, i]) for i in range(count)]
    writes = [pltpu.make_async_copy(held[i], outs[i], sems.at[1, i]) for i in range(count)]
    for copy in reads:
        copy.start()
    for i in range(count):
        reads[i].wait()
        writes[i].start()
    for copy in writes:
        copy.wait()


def local(
    feats, w_spatial, w_temporal, teacher_mid, w_down, w_query, w_key, w_value, w_out, teacher_top
):
    frames = lax.axis_size("tm")
    spaces = lax.axis_size("space")
    devices_all = lax.axis_size("dp") * frames * spaces
    rows, cols, chan = feats.shape[2:]
    half_rows, half_cols, width = teacher_top.shape[2:]
    wc, hc = cols // frames, half_cols // frames
    scale_mid = 1.0 / math.sqrt(rows * cols * devices_all)
    scale_top = 1.0 / math.sqrt(half_rows * half_cols * devices_all)
    dma = pltpu.SemaphoreType.DMA
    group, clips = frames * spaces, lax.axis_size("dp")
    grads = (w_temporal.shape, w_out.shape)
    reduce = clips == 4 and all(r % (32 * group) == 0 and c % 256 == 0 for r, c in grads)
    pieces = [(r // group, c) if reduce else (r, c) for r, c in grads]
    student, gt, go = pl.pallas_call(
        functools.partial(kernel, frames, spaces, clips, reduce, scale_mid, scale_top),
        out_shape=(
            jax.ShapeDtypeStruct((half_rows, frames, hc, width), BF16),
            jax.ShapeDtypeStruct(pieces[0], F32),
            jax.ShapeDtypeStruct(pieces[1], F32),
        ),
        in_specs=[pl.BlockSpec(memory_space=pl.ANY)] * 10,
        out_specs=(pl.BlockSpec(memory_space=pltpu.VMEM),) * 3,
        scratch_shapes=[
            pltpu.VMEM((rows, frames, wc, chan), BF16),
            pltpu.VMEM((3, 3 * chan, chan), BF16),
            pltpu.VMEM(w_temporal.shape, BF16),
            pltpu.VMEM(w_down.shape, BF16),
            pltpu.VMEM(w_query.shape, BF16),
            pltpu.VMEM(w_key.shape, BF16),
            pltpu.VMEM(w_value.shape, BF16),
            pltpu.VMEM(w_out.shape, BF16),
            pltpu.VMEM((rows + 2, frames, wc, chan), BF16),
            pltpu.VMEM((frames, 2 * rows, chan), BF16),
            pltpu.VMEM((frames, 2 * rows, chan), BF16),
            pltpu.VMEM((2, frames, 2 * rows, chan), BF16),
            pltpu.VMEM((rows + 2, frames * wc, 3 * chan), BF16),
            pltpu.VMEM((frames + 2, rows, wc, chan), BF16),
            pltpu.VMEM((chan, (frames + 2) * rows * wc), BF16),
            pltpu.VMEM((frames, rows, wc, chan), BF16),
            pltpu.VMEM((frames, half_rows, hc, width), BF16),
            pltpu.VMEM((2, frames * rows * wc, chan // 2), F32),
            pltpu.VMEM((frames, half_rows, hc, width), BF16),
            dma((8,)),
            dma((4,)),
        ]
        + [dma((frames,))] * 4
        + [dma((frames,))] * 2
        + [dma((frames,))] * 4
        + [dma((4,)), dma((4,))]
        + (sum_scratch(grads[0], group, clips) + sum_scratch(grads[1], group, clips) if reduce else []),
        compiler_params=pltpu.CompilerParams(
            collective_id=0, has_side_effects=True, vmem_limit_bytes=58 * 1024 * 1024
        ),
    )(
        feats.reshape(rows, frames, wc, chan),
        w_spatial.reshape(3, 3 * chan, chan),
        w_temporal,
        teacher_mid.reshape(rows, frames, wc, chan),
        w_down,
        w_query,
        w_key,
        w_value,
        w_out,
        teacher_top.reshape(half_rows, frames, hc, width),
    )
    if reduce:
        student, gt, go = pl.pallas_call(
            hand_over,
            out_shape=tuple(jax.ShapeDtypeStruct(x.shape, x.dtype) for x in (student, gt, go)),
            in_specs=[pl.BlockSpec(memory_space=pl.ANY)] * 3,
            out_specs=(pl.BlockSpec(memory_space=pl.ANY),) * 3,
            scratch_shapes=[pltpu.VMEM(x.shape, x.dtype) for x in (student, gt, go)]
            + [dma((2, 3))],
            compiler_params=pltpu.CompilerParams(vmem_limit_bytes=58 * 1024 * 1024),
        )(student, gt, go)
    else:
        gt = lax.psum_scatter(gt, ("tm", "space"), scatter_dimension=0, tiled=True)
        go = lax.psum_scatter(go, ("tm", "space"), scatter_dimension=0, tiled=True)
        gt, go = lax.psum((gt, go), "dp")
    return (student.reshape(1, 1, half_rows, half_cols, width), gt, go)


def solution(mesh):
    frame = P("dp", "tm", "space", None, None)
    return jax.shard_map(
        local,
        mesh=mesh,
        in_specs=(frame, P(), P(), frame, P(), P(), P(), P(), P(), frame),
        out_specs=(frame, P(("tm", "space"), None), P(("tm", "space"), None)),
        check_vma=False,
    )
```

```python
import functools
import math

import jax
import jax.numpy as jnp
from jax import lax
from jax.experimental import pallas as pl
from jax.experimental.pallas import tpu as pltpu
from jax.sharding import PartitionSpec as P

MESH = pl.DeviceIdType.MESH
F32 = jnp.float32
BF16 = jnp.bfloat16


def dot(a, b):
    return jnp.dot(a, b, preferred_element_type=F32)


class Sum:
    def __init__(self, refs, out, grad, d, me, members, others, spaces):
        (self.part, self.in1, self.half, self.in2, self.quarter, self.in3, self.done,
         self.sem12, self.s3, self.r3, self.s4, self.r4) = refs
        self.out, self.grad, self.d, self.me = out, grad, d, me
        self.members, self.others, self.spaces = members, others, spaces

    def copy(self, src, dst, ssem, rsem, to):
        return pltpu.make_async_remote_copy(
            src_ref=src, dst_ref=dst, send_sem=ssem, recv_sem=rsem,
            device_id=to, device_id_type=MESH,
        )

    def one(self):
        low = lax.rem(self.d, 2)
        return self.copy(self.part.at[1 - low], self.in1, self.sem12.at[0], self.sem12.at[1],
                         {"dp": self.d + 1 - 2 * low})

    def two(self):
        high = self.d // 2
        return self.copy(self.half.at[1 - high], self.in2, self.sem12.at[2], self.sem12.at[3],
                         {"dp": self.d + 2 - 4 * high})

    def three(self, g, f):
        return self.copy(self.quarter.at[g], self.in3.at[f], self.s3.at[g], self.r3.at[f],
                         {"tm": g // self.spaces, "space": lax.rem(g, self.spaces)})

    def four(self, c, f):
        return self.copy(self.done.at[f], self.done.at[f], self.s4.at[c], self.r4.at[f],
                         {"dp": c})

    def first(self):
        _, group, rows, cols = self.part.shape
        split = self.grad.astype(BF16).reshape(group, 2, rows, cols)
        for h in range(2):
            self.part[h] = split[:, h]
        self.one().start()

    def second(self):
        self.one().wait_recv()
        total = self.part[lax.rem(self.d, 2)].astype(F32) + self.in1[...].astype(F32)
        cols = self.half.shape[-1]
        for h in range(2):
            self.half[h] = total[..., h * cols:(h + 1) * cols].astype(BF16)
        self.two().start()

    def third(self):
        self.two().wait_recv()
        total = self.half[self.d // 2].astype(F32) + self.in2[...].astype(F32)
        self.quarter[...] = total.astype(BF16)
        for g in self.members:
            self.three(g, self.me).start()
        self.in3[self.me] = self.quarter[self.me]

    def fourth(self):
        for g in self.members:
            self.three(g, g).wait_recv()
        self.done[self.d] = jnp.sum(self.in3[...].astype(F32), 0).astype(BF16)
        for c in self.others:
            self.four(c, self.d).start()

    def finish(self):
        for c in self.others:
            self.four(c, c).wait_recv()
        count, rows, cols = self.done.shape
        for c in range(count):
            self.out[pl.ds((c % 2) * rows, rows), pl.ds((c // 2) * cols, cols)] = self.done[c].astype(F32)
        self.one().wait_send()
        self.two().wait_send()
        for g in self.members:
            self.three(g, self.me).wait_send()
        for c in self.others:
            self.four(c, self.d).wait_send()


def sum_scratch(shape, group, clips):
    dma = pltpu.SemaphoreType.DMA
    rows, cols = shape[0] // group // 2, shape[1]
    return [
        pltpu.VMEM((2, group, rows, cols), BF16),
        pltpu.VMEM((group, rows, cols), BF16),
        pltpu.VMEM((2, group, rows, cols // 2), BF16),
        pltpu.VMEM((group, rows, cols // 2), BF16),
        pltpu.VMEM((group, rows, cols // 2), BF16),
        pltpu.VMEM((group, rows, cols // 2), BF16),
        pltpu.VMEM((clips, rows, cols // 2), BF16),
        dma((4,)),
        dma((group,)),
        dma((group,)),
        dma((clips,)),
        dma((clips,)),
    ]


def kernel(
    frames, spaces, clips, reduce, scale_mid, scale_top,
    feats, w_sp, w_tm, teach, w_dn, w_q, w_k, w_v, w_o, teach_top,
    student_out, gt_out, go_out,
    home, v_sp, v_tm, v_dn, v_q, v_k, v_v, v_o,
    cells, edge_send, edges, edge_near, shifted, spat, turned, teacher, teacher_top, mid32, stu,
    in_sem, own_sem, fs, fr, es, er, ts, tr, ps, pr_, ss, sr, hs, hr,
    *sums,
):
    t = lax.axis_index("tm")
    s = lax.axis_index("space")
    rows, _, wc, chan = feats.shape
    half_rows, _, hc, width = teach_top.shape
    peers = [lax.rem(t + i, frames) for i in range(1, frames)]
    group = frames * spaces
    me = t * spaces + s
    members = [lax.rem(me + i, group) for i in range(1, group)]
    d = lax.axis_index("dp")
    others = [lax.rem(d + i, clips) for i in range(1, clips)]

    loads = [
        pltpu.make_async_copy(src, dst, in_sem.at[i])
        for i, (src, dst) in enumerate(
            ((feats, home), (w_sp, v_sp), (w_tm, v_tm), (w_dn, v_dn),
             (w_q, v_q), (w_k, v_k), (w_v, v_v), (w_o, v_o))
        )
    ]
    own = [
        pltpu.make_async_copy(feats.at[:, t], cells.at[pl.ds(1, rows), t], own_sem.at[0]),
        pltpu.make_async_copy(teach.at[:, t], teacher.at[t], own_sem.at[1]),
        pltpu.make_async_copy(teach_top.at[:, t], teacher_top.at[t], own_sem.at[2]),
    ]
    barrier = pltpu.get_barrier_semaphore()
    for g in members:
        pl.semaphore_signal(
            barrier, inc=1, device_id={"tm": g // spaces, "space": lax.rem(g, spaces)},
            device_id_type=MESH,
        )
    if reduce:
        for c in others:
            pl.semaphore_signal(barrier, inc=1, device_id={"dp": c}, device_id_type=MESH)

    loads[0].start()

    def send(src, dst, ssem, rsem, u):
        return pltpu.make_async_remote_copy(
            src_ref=src, dst_ref=dst, send_sem=ssem, recv_sem=rsem,
            device_id={"tm": u}, device_id_type=MESH,
        )

    def feats_copy(u, f):
        return send(feats.at[:, u], cells.at[pl.ds(1, rows), f], fs.at[u], fr.at[f], u)

    def edge_copy(u, f):
        return send(edge_send.at[u], edges.at[f], es.at[u], er.at[f], u)

    def teach_copy(u, f):
        return send(teach.at[:, u], teacher.at[f], ts.at[u], tr.at[f], u)

    def top_copy(u, f):
        return send(teach_top.at[:, u], teacher_top.at[f], ps.at[u], pr_.at[f], u)

    def student_copy(u, f):
        return send(stu.at[u], student_out.at[:, f], ss.at[u], sr.at[f], u)

    pl.semaphore_wait(barrier, group - 1 + (clips - 1 if reduce else 0))
    for u in peers:
        feats_copy(u, t).start()
    for copy in own:
        copy.start()
    for load in loads[1:]:
        load.start()

    loads[0].wait()
    for u in range(frames):
        if u > 0:
            left = home[:, u - 1, wc - 8:, :].astype(F32)[:, 7, :]
        else:
            left = jnp.zeros((rows, chan), F32)
        if u < frames - 1:
            right = home[:, u + 1, :8, :].astype(F32)[:, 0, :]
        else:
            right = jnp.zeros((rows, chan), F32)
        edge_send[u] = jnp.concatenate([left, right], 0).astype(BF16)

    for u in peers:
        edge_copy(u, t).start()
    edges[t] = edge_send[t]
    spat[pl.ds(0, 2)] = jnp.zeros((2,) + spat.shape[1:], BF16)

    @pl.when(s == 0)
    def _():
        cells[0] = jnp.zeros(cells.shape[1:], BF16)
        edge_near[0] = jnp.zeros(edges.shape, BF16)

    @pl.when(s == spaces - 1)
    def _():
        cells[rows + 1] = jnp.zeros(cells.shape[1:], BF16)
        edge_near[1] = jnp.zeros(edges.shape, BF16)

    own[0].wait()
    for f in peers:
        edge_copy(f, f).wait_recv()
        feats_copy(f, f).wait_recv()
    for u in peers:
        top_copy(u, t).start()
    for u in peers:
        teach_copy(u, t).start()

    def halo(src, dst, i, j, to):
        return pltpu.make_async_remote_copy(
            src_ref=src, dst_ref=dst, send_sem=hs.at[i], recv_sem=hr.at[j],
            device_id={"space": to}, device_id_type=MESH,
        )

    def up(to):
        return (halo(cells.at[1], cells.at[rows + 1], 0, 0, to),
                halo(edges, edge_near.at[1], 1, 1, to))

    def down(to):
        return (halo(cells.at[rows], cells.at[0], 2, 2, to),
                halo(edges, edge_near.at[0], 3, 3, to))

    @pl.when(s > 0)
    def _():
        for copy in up(s - 1):
            copy.start()

    @pl.when(s < spaces - 1)
    def _():
        for copy in down(s + 1):
            copy.start()

    column = lax.broadcasted_iota(jnp.int32, (frames, wc, chan), 1)

    def shift(row, left, right):
        x = cells[row].astype(F32)
        a = jnp.where(column == 0, left, pltpu.roll(x, 1, 1))
        b = jnp.where(column == wc - 1, right, pltpu.roll(x, wc - 1, 1))
        flat = (frames * wc, chan)
        shifted[row, :, pl.ds(0, chan)] = a.astype(BF16).reshape(flat)
        shifted[row, :, pl.ds(chan, chan)] = cells[row].reshape(flat)
        shifted[row, :, pl.ds(2 * chan, chan)] = b.astype(BF16).reshape(flat)

    def conv(spans):
        count = sum(c for _, c in spans)
        total = None
        for dy in range(3):
            blocks = [
                shifted[pl.ds(first + dy, c)].reshape(c * frames * wc, 3 * chan)
                for first, c in spans
            ]
            block = blocks[0] if len(blocks) == 1 else jnp.concatenate(blocks, 0)
            term = dot(block, v_sp[dy])
            total = term if total is None else total + term
        out = (total / (1.0 + jnp.exp(-total))).astype(BF16)
        out = out.reshape(count, frames, wc, chan)
        places = [first + i for first, c in spans for i in range(c)]
        for i, row in enumerate(places):
            spat[pl.ds(2, frames), row] = out[i]

    side = edges[...].astype(F32)
    for r in range(rows):
        shift(r + 1, side[:, r:r + 1, :], side[:, rows + r:rows + r + 1, :])
    loads[1].wait()
    conv([(1, rows - 2)])

    @pl.when(s < spaces - 1)
    def _():
        for copy in up(s + 1):
            copy.wait_recv()

    @pl.when(s > 0)
    def _():
        for copy in down(s - 1):
            copy.wait_recv()

    side = edge_near[0].astype(F32)
    shift(0, side[:, rows - 1:rows, :], side[:, 2 * rows - 1:2 * rows, :])
    side = edge_near[1].astype(F32)
    shift(rows + 1, side[:, 0:1, :], side[:, rows:rows + 1, :])
    conv([(0, 1), (rows - 1, 1)])

    loads[2].wait()
    half = chan // 2
    n = frames * rows * wc
    total = None
    for k in range(3):
        term = dot(spat[pl.ds(k, frames)].reshape(n, chan), v_tm[pl.ds(k * chan, chan), :])
        total = term if total is None else total + term
    for f in range(frames):
        base = cells[pl.ds(1, rows), f].astype(F32).reshape(rows * wc, chan)
        span = slice(f * rows * wc, (f + 1) * rows * wc)
        mid = (base + total[span]).astype(BF16).astype(F32)
        for h in range(2):
            mid32[h, span, :] = mid[:, h * half:(h + 1) * half]

    loads[3].wait()
    coarse = None
    count = frames * rows * wc // 2
    for b in range(2):
        part = jnp.concatenate(
            [mid32[h, pl.ds(b, count, stride=2), :] for h in range(2)], -1
        ).reshape(frames * half_rows, 2, hc, chan)
        for a in range(2):
            block = part[:, a].reshape(frames * half_rows * hc, chan).astype(BF16)
            term = dot(block, v_dn[a, b])
            coarse = term if coarse is None else coarse + term
    coarse = coarse.astype(BF16)

    for i in range(4, 8):
        loads[i].wait()
    points = half_rows * hc
    query = dot(coarse, v_q[...]).astype(BF16).astype(F32).reshape(frames, points, width)
    key = dot(coarse, v_k[...]).astype(BF16).astype(F32).reshape(frames, points, width)
    value = dot(coarse, v_v[...]).astype(BF16).astype(F32).reshape(frames, points, width)
    scale = 1.0 / math.sqrt(width)
    results = []
    for q in range(frames):
        score = [jnp.sum(query[q] * key[k], -1, keepdims=True) * scale for k in range(q + 1)]
        top = functools.reduce(jnp.maximum, score)
        weight = [jnp.exp(x - top) for x in score]
        total = functools.reduce(jnp.add, weight)
        acc = functools.reduce(jnp.add, [weight[k] * value[k] for k in range(q + 1)])
        results.append(acc / total)
    attended = jnp.concatenate(results, 0).astype(BF16)
    student = (coarse.astype(F32) + dot(attended, v_o[...])).astype(BF16)
    stu[...] = student.reshape(frames, half_rows, hc, width)
    keep = pltpu.make_async_copy(stu.at[t], student_out.at[:, t], own_sem.at[3])
    keep.start()


    turned_top = attended.T
    own[2].wait()
    for f in peers:
        top_copy(f, f).wait_recv()
    diff_top = (
        student.astype(F32) - teacher_top[...].astype(F32).reshape(frames * points, width)
    ).astype(BF16)
    grad_top = dot(turned_top, diff_top) * scale_top
    if reduce:
        top_sum = Sum(sums[12:], go_out, grad_top, d, me, members, others, spaces)
        top_sum.first()
    else:
        go_out[...] = grad_top

    frame = rows * wc
    turned[:, pl.ds(0, 2 * frame)] = jnp.zeros((chan, 2 * frame), BF16)
    for f in range(frames):
        turned[:, pl.ds((f + 2) * frame, frame)] = spat[f + 2].reshape(frame, chan).T
    if reduce:
        top_sum.second()
        top_sum.third()
    own[1].wait()
    for f in peers:
        teach_copy(f, f).wait_recv()
    for u in peers:
        student_copy(u, t).start()
    mid = jnp.concatenate([mid32[0], mid32[1]], -1)
    diff = (mid - teacher[...].astype(F32).reshape(n, chan)).astype(BF16)
    grad = [dot(turned[:, pl.ds(k * frame, n)], diff) for k in range(3)]
    grad = jnp.concatenate(grad, 0) * scale_mid
    if reduce:
        mid_sum = Sum(sums[:12], gt_out, grad, d, me, members, others, spaces)
        mid_sum.first()
        mid_sum.second()
        top_sum.fourth()
        mid_sum.third()
        top_sum.finish()
        mid_sum.fourth()
        mid_sum.finish()
    else:
        gt_out[...] = grad

    keep.wait()
    for u in peers:
        student_copy(u, u).wait_recv()
    for u in peers:
        edge_copy(u, t).wait_send()
        feats_copy(u, t).wait_send()
        teach_copy(u, t).wait_send()
        top_copy(u, t).wait_send()
        student_copy(u, t).wait_send()

    @pl.when(s > 0)
    def _():
        for copy in up(s - 1):
            copy.wait_send()

    @pl.when(s < spaces - 1)
    def _():
        for copy in down(s + 1):
            copy.wait_send()


def hand_over(*refs):
    count = (len(refs) - 1) // 3
    ins, outs, held, sems = refs[:count], refs[count:2 * count], refs[2 * count:-1], refs[-1]
    reads = [pltpu.make_async_copy(ins[i], held[i], sems.at[0, i]) for i in range(count)]
    writes = [pltpu.make_async_copy(held[i], outs[i], sems.at[1, i]) for i in range(count)]
    for copy in reads:
        copy.start()
    for i in range(count):
        reads[i].wait()
        writes[i].start()
    for copy in writes:
        copy.wait()


def local(
    feats, w_spatial, w_temporal, teacher_mid, w_down, w_query, w_key, w_value, w_out, teacher_top
):
    frames = lax.axis_size("tm")
    spaces = lax.axis_size("space")
    devices_all = lax.axis_size("dp") * frames * spaces
    rows, cols, chan = feats.shape[2:]
    half_rows, half_cols, width = teacher_top.shape[2:]
    wc, hc = cols // frames, half_cols // frames
    scale_mid = 1.0 / math.sqrt(rows * cols * devices_all)
    scale_top = 1.0 / math.sqrt(half_rows * half_cols * devices_all)
    dma = pltpu.SemaphoreType.DMA
    group, clips = frames * spaces, lax.axis_size("dp")
    grads = (w_temporal.shape, w_out.shape)
    reduce = clips == 4 and all(r % (32 * group) == 0 and c % 256 == 0 for r, c in grads)
    pieces = [(r // group, c) if reduce else (r, c) for r, c in grads]
    student, gt, go = pl.pallas_call(
        functools.partial(kernel, frames, spaces, clips, reduce, scale_mid, scale_top),
        out_shape=(
            jax.ShapeDtypeStruct((half_rows, frames, hc, width), BF16),
            jax.ShapeDtypeStruct(pieces[0], F32),
            jax.ShapeDtypeStruct(pieces[1], F32),
        ),
        in_specs=[pl.BlockSpec(memory_space=pl.ANY)] * 10,
        out_specs=(pl.BlockSpec(memory_space=pltpu.VMEM),) * 3,
        scratch_shapes=[
            pltpu.VMEM((rows, frames, wc, chan), BF16),
            pltpu.VMEM((3, 3 * chan, chan), BF16),
            pltpu.VMEM(w_temporal.shape, BF16),
            pltpu.VMEM(w_down.shape, BF16),
            pltpu.VMEM(w_query.shape, BF16),
            pltpu.VMEM(w_key.shape, BF16),
            pltpu.VMEM(w_value.shape, BF16),
            pltpu.VMEM(w_out.shape, BF16),
            pltpu.VMEM((rows + 2, frames, wc, chan), BF16),
            pltpu.VMEM((frames, 2 * rows, chan), BF16),
            pltpu.VMEM((frames, 2 * rows, chan), BF16),
            pltpu.VMEM((2, frames, 2 * rows, chan), BF16),
            pltpu.VMEM((rows + 2, frames * wc, 3 * chan), BF16),
            pltpu.VMEM((frames + 2, rows, wc, chan), BF16),
            pltpu.VMEM((chan, (frames + 2) * rows * wc), BF16),
            pltpu.VMEM((frames, rows, wc, chan), BF16),
            pltpu.VMEM((frames, half_rows, hc, width), BF16),
            pltpu.VMEM((2, frames * rows * wc, chan // 2), F32),
            pltpu.VMEM((frames, half_rows, hc, width), BF16),
            dma((8,)),
            dma((4,)),
        ]
        + [dma((frames,))] * 4
        + [dma((frames,))] * 2
        + [dma((frames,))] * 4
        + [dma((4,)), dma((4,))]
        + (sum_scratch(grads[0], group, clips) + sum_scratch(grads[1], group, clips) if reduce else []),
        compiler_params=pltpu.CompilerParams(
            collective_id=0, has_side_effects=True, vmem_limit_bytes=58 * 1024 * 1024
        ),
    )(
        feats.reshape(rows, frames, wc, chan),
        w_spatial.reshape(3, 3 * chan, chan),
        w_temporal,
        teacher_mid.reshape(rows, frames, wc, chan),
        w_down,
        w_query,
        w_key,
        w_value,
        w_out,
        teacher_top.reshape(half_rows, frames, hc, width),
    )
    if reduce:
        student, gt, go = pl.pallas_call(
            hand_over,
            out_shape=tuple(jax.ShapeDtypeStruct(x.shape, x.dtype) for x in (student, gt, go)),
            in_specs=[pl.BlockSpec(memory_space=pl.ANY)] * 3,
            out_specs=(pl.BlockSpec(memory_space=pl.ANY),) * 3,
            scratch_shapes=[pltpu.VMEM(x.shape, x.dtype) for x in (student, gt, go)]
            + [dma((2, 3))],
            compiler_params=pltpu.CompilerParams(vmem_limit_bytes=58 * 1024 * 1024),
        )(student, gt, go)
    else:
        gt = lax.psum_scatter(gt, ("tm", "space"), scatter_dimension=0, tiled=True)
        go = lax.psum_scatter(go, ("tm", "space"), scatter_dimension=0, tiled=True)
        gt, go = lax.psum((gt, go), "dp")
    return (student.reshape(1, 1, half_rows, half_cols, width), gt, go)


def solution(mesh):
    frame = P("dp", "tm", "space", None, None)
    return jax.shard_map(
        local,
        mesh=mesh,
        in_specs=(frame, P(), P(), frame, P(), P(), P(), P(), P(), frame),
        out_specs=(frame, P(("tm", "space"), None), P(("tm", "space"), None)),
        check_vma=False,
    )
```
